256 devices in a mesh: ctx: 32 (over y, z), tp: 8 (over x, core).
Axes of the slice: x: 4, y: 4, z: 8, core: 2. Of those that a mesh axis runs over, the one named last changes fastest.
Arguments:
- queries: bfloat16 [4096, 8192], P('ctx', 'tp'), may hold values from -24 to 24
- new_keys: bfloat16 [4096, 1024], P('ctx', 'tp'), may hold values from -24 to 24
- new_values: bfloat16 [4096, 1024], P('ctx', 'tp'), may hold values from -6 to 6
- store_keys: bfloat16 [512, 128, 1024], P('ctx', None, 'tp'), may hold values from -24 to 24
- store_values: bfloat16 [512, 128, 1024], P('ctx', None, 'tp'), may hold values from -6 to 6
- hit_blocks: int32 [32, 32, 4], P('ctx'), may hold values from 0 to 15, as said below
- hit_counts: int32 [32, 32], P('ctx'), may hold values from 0 to 4, as said below
- new_lengths: int32 [32], P('ctx'), may hold values from 32 to 128, as said below
- out_weight: bfloat16 [8192, 8192], P('tp', 'ctx'), may hold values from -0.0625 to 0.0625
Outputs:
- projected: bfloat16 [4096, 8192], P('tp', 'ctx')
The draws below stay inside these ranges and needn't reach their ends.
Inputs may be any that keep to these rules, and one draw needn't show every extreme that they name: `hit_blocks`: entries of one list are distinct block numbers of that holder's store; padded entries are valid numbers too. `hit_counts`: for every sequence some holder has exactly 4. `new_lengths`: some sequence uses all 128 slots.
All inputs are finite; a program needn't handle non-finite values.
Results may differ from the reference program's by a relative error of at most 0.015.
Values may be sent and summed in bfloat16 or wider, within the bound.
No kernel may reach another device: no remote copies, remote signals or barrier semaphores. Data moves between devices by JAX's collectives and lax.ppermute only.
A program may use at most 128 MiB of HBM per device.

```python
import jax
import jax.numpy as jnp
from jax import lax

D = 8192
HEADS = 64
KV_HEADS = 8
HEAD = 128
BLOCK = 128
TOK_DEV = 128
MOST = 4
STORE_DEV = 16
TOKENS = 4096
BLOCKS = 512
N_CTX = 32


def draw_queries(key, part):
    inner = jax.random.fold_in(key, 1)
    base = 2.0 * jax.random.normal(inner, (TOKENS, HEADS, HEAD), jnp.float32)
    out = jnp.clip(base, -24.0, 24.0)
    return out.reshape(TOKENS, HEADS * HEAD).astype(jnp.bfloat16)


def draw_new_keys(key, part):
    inner = jax.random.fold_in(key, 2)
    base = jax.random.normal(inner, (TOKENS, KV_HEADS, HEAD), jnp.float32)
    out = jnp.clip(base, -24.0, 24.0)
    return out.reshape(TOKENS, KV_HEADS * HEAD).astype(jnp.bfloat16)


def draw_store_keys(key, part):
    inner = jax.random.fold_in(key, 3)
    base = jax.random.normal(inner, (BLOCKS, BLOCK, KV_HEADS, HEAD), jnp.float32)
    out = jnp.clip(base, -24.0, 24.0)
    return out.reshape(BLOCKS, BLOCK, KV_HEADS * HEAD).astype(jnp.bfloat16)


def draw_hit_blocks(key, part):
    key = jax.random.fold_in(key, 4)
    keys = jax.random.split(key, N_CTX * N_CTX)
    lists = jax.vmap(lambda k: jax.random.permutation(k, STORE_DEV)[:MOST])(keys)
    return lists.reshape(N_CTX, N_CTX, MOST).astype(jnp.int32)


def draw_hit_counts(key, part):
    key = jax.random.fold_in(key, 7)
    base = jax.random.randint(jax.random.fold_in(key, 1), (N_CTX, N_CTX), 0, MOST + 1)
    chosen = jax.random.randint(jax.random.fold_in(key, 2), (N_CTX,), 0, N_CTX)
    holders = jnp.arange(N_CTX, dtype=jnp.int32)[:, None]
    return jnp.where(holders == chosen[None, :], MOST, base).astype(jnp.int32)


def draw_new_lengths(key, part):
    key = jax.random.fold_in(key, 8)
    base = jax.random.randint(jax.random.fold_in(key, 1), (N_CTX,), TOK_DEV // 4, TOK_DEV + 1)
    chosen = jax.random.randint(jax.random.fold_in(key, 2), (), 0, N_CTX)
    return jnp.where(jnp.arange(N_CTX, dtype=jnp.int32) == chosen, TOK_DEV, base).astype(jnp.int32)


def levels(key, shape, pieces, low, largest):
    factor_of = 1.0
    for position, shards_of in pieces:
        steps = jax.random.uniform(jax.random.fold_in(jax.random.fold_in(key, 6), position), (shards_of,), jnp.float32, low / len(pieces), largest / len(pieces))
        factor_of = factor_of * jnp.repeat(jnp.exp(steps), shape[position] // shards_of).reshape((-1,) + (1,) * (len(shape) - 1 - position))
    return factor_of


def centred(stream_key, extent, scale, most, cuts=(), held_as=jnp.bfloat16):
    array = jax.random.normal(stream_key, extent, jnp.float32) * scale
    if len(cuts) > 0:
        array = levels(stream_key, extent, cuts, -0.22, 0.18) * array
    return jnp.clip(array, min=-most, max=most).astype(held_as)


def setup_inputs(seed: int = 0) -> dict:
    splits = jax.random.split(jax.random.key(seed), 10)
    queries = draw_queries(jax.random.fold_in(splits[9], 71), 0)
    new_keys = draw_new_keys(jax.random.fold_in(splits[9], 71), 0)
    new_values = centred(splits[2], (TOKENS, KV_HEADS * HEAD), 1.0, 6.0, ((0, 32), (1, 8)))
    store_keys = draw_store_keys(jax.random.fold_in(splits[9], 71), 0)
    store_values = centred(splits[4], (BLOCKS, BLOCK, KV_HEADS * HEAD), 1.0, 6.0, ((0, 32), (2, 8)))
    hit_blocks = draw_hit_blocks(jax.random.fold_in(splits[9], 71), 0)
    hit_counts = draw_hit_counts(jax.random.fold_in(splits[9], 71), 0)
    new_lengths = draw_new_lengths(jax.random.fold_in(splits[9], 71), 0)
    out_weight = centred(splits[8], (HEADS * HEAD, D), (HEADS * HEAD) ** -0.5, 0.0625, ((0, 8), (1, 32)))
    return {"queries": queries, "new_keys": new_keys, "new_values": new_values, "store_keys": store_keys, "store_values": store_values, "hit_blocks": hit_blocks, "hit_counts": hit_counts, "new_lengths": new_lengths, "out_weight": out_weight}


NEG = -1e30


def group_part(q, keys, values, mask):
    scale = q.shape[-1] ** -0.5
    s = jnp.einsum('tcgd,kcd->cgtk', q.astype(jnp.float32), keys.astype(jnp.float32)) * scale
    s = jnp.where(mask, s, NEG)
    m = jnp.max(s, axis=-1)
    p = jnp.where(mask, jnp.exp(s - m[..., None]), 0.0)
    l = jnp.sum(p, axis=-1)
    pw = lax.optimization_barrier(p.astype(jnp.bfloat16)).astype(jnp.float32)
    o = jnp.einsum('cgtk,kcd->tcgd', pw, values.astype(jnp.float32)).astype(jnp.bfloat16)
    return m, l, o


def combine(carry, part):
    big_m, big_l, acc = carry
    m, l, o = part
    new_m = jnp.maximum(big_m, m)
    a = jnp.exp(big_m - new_m)
    b = jnp.exp(m - new_m)
    at = jnp.transpose(a, (2, 0, 1))[..., None]
    bt = jnp.transpose(b, (2, 0, 1))[..., None]
    return new_m, big_l * a + l * b, acc * at + o.astype(jnp.float32) * bt


def reference(queries, new_keys, new_values, store_keys, store_values, hit_blocks, hit_counts, new_lengths, out_weight):
    group = HEADS // KV_HEADS
    rows_idx = jnp.arange(TOK_DEV, dtype=jnp.int32)

    def one_seq(seq):
        start = (seq * TOK_DEV).astype(jnp.int32)
        q = lax.dynamic_slice_in_dim(queries, start, TOK_DEV, 0).reshape(TOK_DEV, KV_HEADS, group, HEAD)
        keys_new = lax.dynamic_slice_in_dim(new_keys, start, TOK_DEV, 0).reshape(TOK_DEV, KV_HEADS, HEAD)
        vals_new = lax.dynamic_slice_in_dim(new_values, start, TOK_DEV, 0).reshape(TOK_DEV, KV_HEADS, HEAD)
        causal = rows_idx[:, None] >= rows_idx[None, :]
        m, l, o = group_part(q, keys_new, vals_new, causal)
        carry = (m, l, o.astype(jnp.float32))
        live_pos = jnp.arange(MOST * BLOCK, dtype=jnp.int32) // BLOCK

        def step(carry, holder):
            blocks = (holder * STORE_DEV + hit_blocks[holder, seq]).astype(jnp.int32)
            keys = store_keys[blocks].reshape(MOST * BLOCK, KV_HEADS, HEAD)
            vals = store_values[blocks].reshape(MOST * BLOCK, KV_HEADS, HEAD)
            mask = jnp.broadcast_to((live_pos < hit_counts[holder, seq])[None, :], (TOK_DEV, MOST * BLOCK))
            return combine(carry, group_part(q, keys, vals, mask)), None

        carry, unused = lax.scan(step, carry, jnp.arange(N_CTX, dtype=jnp.int32))
        big_m, big_l, acc = carry
        attended = acc / jnp.transpose(big_l, (2, 0, 1))[..., None]
        attended = attended.reshape(TOK_DEV, HEADS * HEAD)
        attended = jnp.where((rows_idx < new_lengths[seq])[:, None], attended, 0.0)
        return attended.astype(jnp.bfloat16)

    head_out = lax.map(one_seq, jnp.arange(N_CTX, dtype=jnp.int32)).reshape(TOKENS, HEADS * HEAD)
    return jnp.dot(head_out, out_weight, preferred_element_type=jnp.float32).astype(jnp.bfloat16)
```

```python
import functools

import jax
import jax.numpy as jnp
from jax import lax
from jax.experimental import pallas as pl
from jax.experimental.pallas import tpu as pltpu
from jax.sharding import PartitionSpec as P

HEAD = 128
BLOCK = 128
MOST = 4
TOK = 128
GROUP = 8
ROWS = GROUP * TOK
STORE = 16
NY = 4
NZ = 8
NX = 4
STATS = 16
PART = HEAD + STATS
NEG = -1e30
SCALE2 = 1.4426950408889634 * HEAD**-0.5
VMEM_BYTES = 44 * 1024 * 1024
F32 = jnp.float32
BF16 = jnp.bfloat16


def pick(seq, n_seqs, hits, k_refs, v_refs, kcat, vcat):
    pos = jnp.int32(0)
    for hit, k_ref, v_ref in zip(hits, k_refs, v_refs):
        count = hit[1, seq]
        for j in range(MOST):
            block = hit[0, seq * MOST + j]

            @pl.when(j < count)
            def _():
                at = pos + j
                kcat[at] = k_ref[block]
                vcat[at] = v_ref[block]

        pos = pos + count
    return pos


def heads_down(q):
    return jnp.concatenate([q[:, g * HEAD : (g + 1) * HEAD] for g in range(q.shape[1] // HEAD)], axis=0)


def scores(k, q):
    return lax.dot_general(k, q, (((1,), (1,)), ((), ())), preferred_element_type=F32)


def fold8(s):
    return jnp.max(s.reshape(s.shape[0] // 8, 8, s.shape[1]), axis=0)


def one_sequence(q, count, kcat, vcat, s_scr, m_scr, acc, new_kv):
    m_scr[...] = jnp.full_like(m_scr, NEG)
    acc[...] = jnp.zeros_like(acc)
    pairs = count // 2
    odd = count - 2 * pairs

    def first(i, carry):
        k = kcat[pl.ds(2 * i, 2)].reshape(2 * BLOCK, HEAD)
        s = scores(k, q)
        s_scr[pl.ds(2 * i, 2)] = s.reshape(2, BLOCK, s.shape[1])
        m_scr[...] = jnp.maximum(m_scr[...], fold8(s))
        return carry

    lax.fori_loop(0, pairs, first, 0)

    @pl.when(odd == 1)
    def _():
        s = scores(kcat[2 * pairs], q)
        s_scr[2 * pairs] = s
        m_scr[...] = jnp.maximum(m_scr[...], fold8(s))

    s_new = None
    if new_kv is not None:
        s_new = scores(new_kv[0], q)
        key = lax.broadcasted_iota(jnp.int32, s_new.shape, 0)
        tok = lax.broadcasted_iota(jnp.int32, s_new.shape, 1) % TOK
        s_new = jnp.where(key <= tok, s_new, NEG)
        s_scr[STORE] = s_new
        m_scr[...] = jnp.maximum(m_scr[...], fold8(s_new))

    m = (jnp.max(m_scr[...], axis=0, keepdims=True) * SCALE2).astype(BF16).astype(F32)

    def weigh(s, v):
        p = jnp.exp2(s * SCALE2 - m).astype(BF16)
        v = jnp.concatenate([v, jnp.ones((STATS, v.shape[1]), BF16)], axis=0)
        acc[...] += jnp.dot(v, p, preferred_element_type=F32)

    def second(i, carry):
        s = s_scr[pl.ds(2 * i, 2)].reshape(2 * BLOCK, s_scr.shape[2])
        weigh(s, jnp.concatenate([vcat[2 * i], vcat[2 * i + 1]], axis=1))
        return carry

    lax.fori_loop(0, pairs, second, 0)

    @pl.when(odd == 1)
    def _():
        weigh(s_scr[2 * pairs], vcat[2 * pairs])

    if new_kv is not None:
        weigh(s_scr[STORE], new_kv[1])
    return m


def stat_rows(m, l):
    high = l.astype(BF16).astype(F32)
    row = lax.broadcasted_iota(jnp.int32, (STATS, m.shape[1]), 0)
    zero = jnp.zeros((STATS, m.shape[1]), F32)
    out = jnp.where(row == 0, m, zero)
    out = jnp.where(row == 1, high, out)
    return jnp.where(row == 2, l - high, out).astype(BF16)


def attend_kernel(n_seqs, n_halves, with_new, *refs):
    seq_ref, refs = refs[0], refs[1:]
    hits, refs = refs[:NY], refs[NY:]
    q_refs, refs = refs[: n_seqs * n_halves], refs[n_seqs * n_halves :]
    k_refs, refs = refs[:NY], refs[NY:]
    v_refs, refs = refs[:NY], refs[NY:]
    new_kv = None
    if with_new:
        new_kv, refs = (refs[0][...], refs[1][...]), refs[2:]
    outs, refs = refs[:n_seqs], refs[n_seqs:]
    kcat, vcat, s_scr, m_scr, acc = refs
    for n in range(n_seqs):
        mine = q_refs[n * n_halves : (n + 1) * n_halves]
        q = jnp.concatenate([heads_down(r[...]) for r in mine], axis=0)
        count = pick(seq_ref[n], n_seqs, hits, k_refs, v_refs, kcat, vcat)
        m = one_sequence(q, count, kcat, vcat, s_scr, m_scr, acc, new_kv)
        outs[n][0:HEAD, :] = acc[0:HEAD, :].astype(BF16)
        outs[n][HEAD:PART, :] = stat_rows(m, acc[HEAD : HEAD + 1, :])


def attend(seqs, hits, qs, n_halves, keys, values, new_kv=()):
    n_seqs = len(qs) // n_halves
    smem = pl.BlockSpec(memory_space=pltpu.SMEM)
    vmem = pl.BlockSpec(memory_space=pltpu.VMEM)
    work = n_seqs * 8
    return pl.pallas_call(
        functools.partial(attend_kernel, n_seqs, n_halves, len(new_kv) > 0),
        out_shape=[jax.ShapeDtypeStruct((PART, ROWS), BF16)] * n_seqs,
        in_specs=[smem] * (1 + NY) + [vmem] * (len(qs) + 2 * NY + len(new_kv)),
        out_specs=[vmem] * n_seqs,
        scratch_shapes=[
            pltpu.VMEM((STORE, BLOCK, HEAD), BF16),
            pltpu.VMEM((STORE, HEAD, BLOCK), BF16),
            pltpu.VMEM((STORE + 1, BLOCK, ROWS), F32),
            pltpu.VMEM((8, ROWS), F32),
            pltpu.VMEM((PART, ROWS), F32),
        ],
        compiler_params=pltpu.CompilerParams(vmem_limit_bytes=VMEM_BYTES),
        cost_estimate=pl.CostEstimate(
            flops=work * 4 * BLOCK * ROWS * HEAD,
            bytes_accessed=5 * 2**20,
            transcendentals=work * BLOCK * ROWS,
        ),
    )(seqs, *hits, *qs, *keys, *values, *new_kv)


def parts_of(x):
    x = x.astype(F32)
    m = x[HEAD : HEAD + 1]
    l = x[HEAD + 1 : HEAD + 2] + x[HEAD + 2 : HEAD + 3]
    return x[0:HEAD], m, l


def merge(parts):
    top = functools.reduce(jnp.maximum, [m for _, m, _ in parts])
    weights = [jnp.exp2(m - top) for _, m, _ in parts]
    o = sum(w * o for w, (o, _, _) in zip(weights, parts))
    l = sum(w * l for w, (_, _, l) in zip(weights, parts))
    return o, top, l


def relay_kernel(halves, own_a, got_a, own_b, got_b, out_a, out_b):
    half = ROWS // 2
    for own, got, out, low in ((own_a, got_a, out_a, True), (own_b, got_b, out_b, False)):
        if halves:
            cols = slice(0, half) if low else slice(half, ROWS)
            rest = slice(half, ROWS) if low else slice(0, half)
            out[:, rest] = own[:, rest]
        else:
            cols = slice(0, ROWS)
        o, m, l = merge([parts_of(own[:, cols]), parts_of(got[...])])
        out[0:HEAD, cols] = o.astype(BF16)
        out[HEAD:PART, cols] = stat_rows(m, l)


def relay(halves, own_a, got_a, own_b, got_b):
    vmem = pl.BlockSpec(memory_space=pltpu.VMEM)
    return pl.pallas_call(
        functools.partial(relay_kernel, halves),
        out_shape=[jax.ShapeDtypeStruct((PART, ROWS), BF16)] * 2,
        in_specs=[vmem] * 4,
        out_specs=[vmem] * 2,
        compiler_params=pltpu.CompilerParams(vmem_limit_bytes=VMEM_BYTES),
        cost_estimate=pl.CostEstimate(flops=8 * PART * ROWS, bytes_accessed=2 * 2**20, transcendentals=4 * ROWS),
    )(own_a, got_a, own_b, got_b)


def finish_kernel(length, own, left, right, out):
    o, _, l = merge([parts_of(own[...]), parts_of(left[...]), parts_of(right[...])])
    attended = o / l
    tok = lax.broadcasted_iota(jnp.int32, attended.shape, 1) % TOK
    attended = jnp.where(tok < length[0], attended, 0.0)
    for g in range(GROUP):
        out[:, g * HEAD : (g + 1) * HEAD] = attended[:, g * TOK : (g + 1) * TOK].T.astype(BF16)


def finish(length, own, left, right):
    vmem = pl.BlockSpec(memory_space=pltpu.VMEM)
    return pl.pallas_call(
        finish_kernel,
        out_shape=jax.ShapeDtypeStruct((TOK, ROWS), BF16),
        in_specs=[pl.BlockSpec(memory_space=pltpu.SMEM)] + [vmem] * 3,
        out_specs=vmem,
        compiler_params=pltpu.CompilerParams(vmem_limit_bytes=VMEM_BYTES),
        cost_estimate=pl.CostEstimate(flops=8 * PART * ROWS, bytes_accessed=2**20, transcendentals=4 * ROWS),
    )(length, own, left, right)


def along_z(x, k):
    return lax.ppermute(x, "ctx", [(y * NZ + z, y * NZ + (z + k) % NZ) for y in range(NY) for z in range(NZ)])


def along_y(x, k):
    return lax.ppermute(x, "ctx", [(y * NZ + z, (y + k) % NY * NZ + z) for y in range(NY) for z in range(NZ)])


def along_x(x, k):
    return lax.ppermute(x, "tp", [(2 * i + c, 2 * ((i + k) % NX) + c) for i in range(NX) for c in range(2)])


def at(x, i):
    return lax.dynamic_index_in_dim(x, i, 0, keepdims=False)


def to_tiles(tile, y, z, t):
    got = []
    for r in range(NY):
        piece = at(tile, (y - r - z) % NY)
        pairs = []
        for yy in range(NY):
            for zz in range(NZ):
                for tt in range(2 * NX):
                    source = (yy * NZ + zz) * 2 * NX + tt
                    target = (yy * NZ + tt) * 2 * NX + 2 * ((r + zz) % NY) + zz // 4
                    pairs.append((source, target))
        got.append(lax.ppermute(piece, ("ctx", "tp"), pairs))
    turned = [got[(-j) % NY] for j in range(NY)]
    both = jnp.concatenate(turned + turned, axis=0)
    start = (-(t // 2)) % NY
    return lax.dynamic_slice_in_dim(both, start * TOK, NY * TOK, 0)


def shards(
    queries,
    new_keys,
    new_values,
    store_keys,
    store_values,
    hit_blocks,
    hit_counts,
    new_lengths,
    out_weight,
):
    me = lax.axis_index("ctx")
    t = lax.axis_index("tp")
    y, z = me // NZ, me % NZ
    x, core = t // 2, t % 2

    weights = lax.all_gather(
        out_weight,
        "ctx",
        axis=0,
        tiled=False,
        axis_index_groups=[[yy * NZ + zz for zz in range(NZ)] for yy in range(NY)],
    )

    hits = jnp.concatenate(
        [hit_blocks.reshape(1, -1), jnp.pad(hit_counts, ((0, 0), (0, 128 - hit_counts.shape[1])))], axis=0
    )
    keys, values = store_keys, jnp.swapaxes(store_values, 1, 2)

    keys_l, keys_r = along_y(keys, 1), along_y(keys, -1)
    hits_l, hits_r, hits_f = along_y(hits, 1), along_y(hits, -1), along_y(hits, 2)
    values_l, values_r = along_y(values, 1), along_y(values, -1)
    keys_f, values_f = along_y(keys_l, 1), along_y(values_r, -1)
    all_hits = [hits, hits_l, hits_r, hits_f]
    all_keys = [keys, keys_l, keys_r, keys_f]
    all_values = [values, values_l, values_r, values_f]

    half = ROWS // 2
    q_up = [queries]
    q_down = [queries]
    for _ in range(3):
        q_up.append(along_z(q_up[-1], -1))
        q_down.append(along_z(q_down[-1], 1))
    q_far = [along_z(q_down[3][:, :half], 1), along_z(q_up[3][:, half:], -1)]

    def number(*places):
        return jnp.stack([y * NZ + (z + d) % NZ for d in places]).astype(jnp.int32)

    run = functools.partial(attend, hits=all_hits, keys=all_keys, values=all_values)
    (far,) = run(number(4), qs=q_far, n_halves=2)
    got_l, got_r = along_z(far[:, :half], 1), along_z(far[:, half:], -1)
    for d in (3, 2, 1):
        up, down = run(number(d, -d), qs=[q_up[d], q_down[d]], n_halves=1)
        to_right, to_left = relay(d == 3, up, got_l, down, got_r)
        got_l, got_r = along_z(to_right, 1), along_z(to_left, -1)
    (own,) = run(number(0), qs=[queries], n_halves=1, new_kv=(new_keys, new_values.T))
    head_out = finish(new_lengths, own, got_l, got_r)

    rows = jnp.concatenate([head_out, along_y(head_out, 1), along_y(head_out, 2), along_y(head_out, 3)], axis=0)
    pairs = weights.reshape(NX, 2, *out_weight.shape)
    other = lax.dynamic_index_in_dim(pairs, 1 - core, 1, keepdims=False)
    mine = lax.dynamic_index_in_dim(pairs, core, 1, keepdims=False)
    form = "rk,xkc->xrc"
    sent = jnp.einsum(form, rows, other, preferred_element_type=F32).astype(BF16)
    swapped = lax.ppermute(sent, "tp", [(i, i ^ 1) for i in range(2 * NX)])
    summed = jnp.einsum(form, rows, mine, preferred_element_type=F32) + swapped.astype(F32)
    thin = summed.astype(BF16)
    total = at(summed, x)
    for k in range(1, NX):
        total = total + along_x(at(thin, (x + k) % NX), k).astype(F32)
    tile = total.astype(BF16).reshape(NY, TOK, out_weight.shape[1])
    return to_tiles(tile, y, z, t)


def solution(mesh):
    return jax.shard_map(
        shards,
        mesh=mesh,
        in_specs=(
            P("ctx", "tp"),
            P("ctx", "tp"),
            P("ctx", "tp"),
            P("ctx", None, "tp"),
            P("ctx", None, "tp"),
            P("ctx", None, None),
            P("ctx", None),
            P("ctx"),
            P("tp", "ctx"),
        ),
        out_specs=P("tp", "ctx"),
        check_vma=False,
    )
```

```python
import functools

import jax
import jax.numpy as jnp
from jax import lax
from jax.experimental import pallas as pl
from jax.experimental.pallas import tpu as pltpu
from jax.sharding import PartitionSpec as P

HEAD = 128
BLOCK = 128
MOST = 4
TOK = 128
GROUP = 8
ROWS = GROUP * TOK
STORE = 16
NY = 4
NZ = 8
NX = 4
STATS = 16
PART = HEAD + STATS
PAIR = 2 * BLOCK
CHUNK = 8
TAILS = (2, 4, 8)
NEG = -1e30
SCALE2 = 1.4426950408889634 * HEAD**-0.5
VMEM_BYTES = 44 * 1024 * 1024
F32 = jnp.float32
BF16 = jnp.bfloat16


def heads_down(q):
    return jnp.concatenate([q[:, g * HEAD : (g + 1) * HEAD] for g in range(q.shape[1] // HEAD)], axis=0)


def scores(k, q):
    return lax.dot_general(k, q, (((1,), (1,)), ((), ())), preferred_element_type=F32)


def fold8(s):
    return jnp.max(s.reshape(s.shape[0] // 8, 8, s.shape[1]), axis=0)


def stat_rows(m, l):
    high = l.astype(BF16).astype(F32)
    row = lax.broadcasted_iota(jnp.int32, (STATS, m.shape[1]), 0)
    zero = jnp.zeros((STATS, m.shape[1]), F32)
    out = jnp.where(row == 0, m, zero)
    out = jnp.where(row == 1, high, out)
    return jnp.where(row == 2, l - high, out).astype(BF16)


def live_copies(seq, slot, hits, stores, far, kv, sems, act):
    pos = jnp.int32(0)
    for h, hit in enumerate(hits):
        count = hit[1, seq]
        for j in range(MOST):
            block = hit[0, seq * MOST + j]

            def copy(ref, row, h=h, j=j, pos=pos):
                source = ref.at[pl.ds(pl.multiple_of(row * PAIR, PAIR), PAIR), :]
                act(pltpu.make_async_copy(source, kv.at[slot, pos + j], sems.at[slot, h * MOST + j]))

            if h < len(stores):

                @pl.when(j < count)
                def _(copy=copy, ref=stores[h], block=block):
                    copy(ref, block)

            else:

                @pl.when((j < count) & (block < STORE // 2))
                def _(copy=copy, ref=far[0], block=block):
                    copy(ref, block)

                @pl.when((j < count) & (block >= STORE // 2))
                def _(copy=copy, ref=far[1], block=block):
                    copy(ref, block - STORE // 2)

        pos = pos + count
    return pos


def attend_kernel(n_seqs, n_halves, with_new, *refs):
    seq_ref, refs = refs[0], refs[1:]
    hits, refs = refs[:NY], refs[NY:]
    q_refs, refs = refs[: n_seqs * n_halves], refs[n_seqs * n_halves :]
    stores, far, refs = refs[:3], refs[3:5], refs[5:]
    new_kv = None
    if with_new:
        new_kv, refs = refs[0], refs[1:]
    out, kv, q_scr, s_scr, m_scr, acc, sems = refs
    copies = functools.partial(live_copies, hits=hits, stores=stores, far=far, kv=kv, sems=sems)
    for n in range(n_seqs):
        copies(seq_ref[n], n, act=lambda c: c.start())
    for n in range(n_seqs):
        mine = q_refs[n * n_halves : (n + 1) * n_halves]
        q_scr[n] = jnp.concatenate([heads_down(r[...]) for r in mine], axis=0)

    def one(n, carry):
        count = copies(seq_ref[n], n, act=lambda c: c.wait())
        full = count // CHUNK
        tail = count - full * CHUNK

        def blank(i, carry):
            kv[n, i, HEAD:PAIR, :] = jnp.zeros((HEAD, BLOCK), BF16)
            return carry

        lax.fori_loop(count, jnp.minimum(count + CHUNK, STORE), blank, 0)

        def each(step):
            lax.fori_loop(0, full, lambda i, c: (step(i * CHUNK, CHUNK, False), c)[1], 0)
            low = 0
            for size in TAILS:

                @pl.when((tail > low) & (tail <= size))
                def _(size=size):
                    step(full * CHUNK, size, True)

                low = size

        q = q_scr[n]
        m_scr[...] = jnp.full_like(m_scr, NEG)
        acc[...] = jnp.zeros_like(acc)

        def first(base, size, masked):
            k = kv[n, pl.ds(base, size)][:, 0:BLOCK, :].reshape(size * BLOCK, HEAD)
            s = scores(k, q)
            if masked:
                key = lax.broadcasted_iota(jnp.int32, s.shape, 0)
                s = jnp.where(key < tail * BLOCK, s, NEG)
            s_scr[pl.ds(base, size)] = s.reshape(size, BLOCK, ROWS)
            m_scr[...] = jnp.maximum(m_scr[...], fold8(s))

        each(first)
        if with_new:
            s = scores(new_kv[0:BLOCK, :], q)
            key = lax.broadcasted_iota(jnp.int32, s.shape, 0)
            tok = lax.broadcasted_iota(jnp.int32, s.shape, 1) % TOK
            s = jnp.where(key <= tok, s, NEG)
            s_scr[STORE] = s
            m_scr[...] = jnp.maximum(m_scr[...], fold8(s))

        m = (jnp.max(m_scr[...], axis=0, keepdims=True) * SCALE2).astype(BF16).astype(F32)

        def weigh(s, v):
            p = jnp.exp2(s * SCALE2 - m).astype(BF16)
            v = jnp.concatenate([v, jnp.ones((STATS, v.shape[1]), BF16)], axis=0)
            acc[...] += jnp.dot(v, p, preferred_element_type=F32)

        def second(base, size, masked):
            s = s_scr[pl.ds(base, size)].reshape(size * BLOCK, ROWS)
            weigh(s, jnp.concatenate([kv[n, base + i][BLOCK:PAIR, :] for i in range(size)], axis=1))

        each(second)
        if with_new:
            weigh(s_scr[STORE], new_kv[BLOCK:PAIR, :])
        out[n, 0:HEAD, :] = acc[0:HEAD, :].astype(BF16)
        out[n, HEAD:PART, :] = stat_rows(m, acc[HEAD : HEAD + 1, :])
        return carry

    lax.fori_loop(0, n_seqs, one, 0)


def attend(seqs, hits, qs, n_halves, stores, far, new_kv=()):
    n_seqs = len(qs) // n_halves
    smem = pl.BlockSpec(memory_space=pltpu.SMEM)
    vmem = pl.BlockSpec(memory_space=pltpu.VMEM)
    anywhere = pl.BlockSpec(memory_space=pl.ANY)
    work = n_seqs * 8
    return pl.pallas_call(
        functools.partial(attend_kernel, n_seqs, n_halves, len(new_kv) > 0),
        out_shape=jax.ShapeDtypeStruct((n_seqs, PART, ROWS), BF16),
        in_specs=[smem] * (1 + NY) + [vmem] * len(qs) + [anywhere] * 5 + [vmem] * len(new_kv),
        out_specs=vmem,
        scratch_shapes=[
            pltpu.VMEM((n_seqs, STORE, PAIR, HEAD), BF16),
            pltpu.VMEM((n_seqs, ROWS, HEAD), BF16),
            pltpu.VMEM((STORE + 1, BLOCK, ROWS), F32),
            pltpu.VMEM((8, ROWS), F32),
            pltpu.VMEM((PART, ROWS), F32),
            pltpu.SemaphoreType.DMA((n_seqs, STORE)),
        ],
        compiler_params=pltpu.CompilerParams(vmem_limit_bytes=VMEM_BYTES),
        cost_estimate=pl.CostEstimate(
            flops=work * 4 * BLOCK * ROWS * HEAD,
            bytes_accessed=5 * 2**20,
            transcendentals=work * BLOCK * ROWS,
        ),
    )(seqs, *hits, *qs, *stores, *far, *new_kv)


def parts_of(x):
    x = x.astype(F32)
    m = x[HEAD : HEAD + 1]
    l = x[HEAD + 1 : HEAD + 2] + x[HEAD + 2 : HEAD + 3]
    return x[0:HEAD], m, l


def merge(parts):
    top = functools.reduce(jnp.maximum, [m for _, m, _ in parts])
    weights = [jnp.exp2(m - top) for _, m, _ in parts]
    o = sum(w * o for w, (o, _, _) in zip(weights, parts))
    l = sum(w * l for w, (_, _, l) in zip(weights, parts))
    return o, top, l


def relay_kernel(halves, own, got_a, got_b, out_a, out_b):
    half = ROWS // 2
    for n, (got, out) in enumerate(((got_a, out_a), (got_b, out_b))):
        cols = slice(0, ROWS)
        if halves:
            cols = slice(n * half, (n + 1) * half)
            rest = slice((1 - n) * half, (2 - n) * half)
            out[:, rest] = own[n, :, rest]
        o, m, l = merge([parts_of(own[n, :, cols]), parts_of(got[...])])
        out[0:HEAD, cols] = o.astype(BF16)
        out[HEAD:PART, cols] = stat_rows(m, l)


def relay(halves, own, got_a, got_b):
    vmem = pl.BlockSpec(memory_space=pltpu.VMEM)
    return pl.pallas_call(
        functools.partial(relay_kernel, halves),
        out_shape=[jax.ShapeDtypeStruct((PART, ROWS), BF16)] * 2,
        in_specs=[vmem] * 3,
        out_specs=[vmem] * 2,
        compiler_params=pltpu.CompilerParams(vmem_limit_bytes=VMEM_BYTES),
        cost_estimate=pl.CostEstimate(flops=8 * PART * ROWS, bytes_accessed=2 * 2**20, transcendentals=4 * ROWS),
    )(own, got_a, got_b)


def finish_kernel(new, own, left, right, out):
    o, _, l = merge([parts_of(own[0]), parts_of(left[...]), parts_of(right[...])])
    attended = o / l
    tok = lax.broadcasted_iota(jnp.int32, attended.shape, 1) % TOK
    length = new[PAIR : PAIR + STATS, :].astype(F32)[0:1, 0:1]
    attended = jnp.where(tok.astype(F32) < length, attended, 0.0)
    for g in range(GROUP):
        out[:, g * HEAD : (g + 1) * HEAD] = attended[:, g * TOK : (g + 1) * TOK].T.astype(BF16)


def finish(new, own, left, right):
    vmem = pl.BlockSpec(memory_space=pltpu.VMEM)
    return pl.pallas_call(
        finish_kernel,
        out_shape=jax.ShapeDtypeStruct((TOK, ROWS), BF16),
        in_specs=[vmem] * 4,
        out_specs=vmem,
        compiler_params=pltpu.CompilerParams(vmem_limit_bytes=VMEM_BYTES),
        cost_estimate=pl.CostEstimate(flops=8 * PART * ROWS, bytes_accessed=2**20, transcendentals=4 * ROWS),
    )(new, own, left, right)


def along_z(x, k):
    return lax.ppermute(x, "ctx", [(y * NZ + z, y * NZ + (z + k) % NZ) for y in range(NY) for z in range(NZ)])


def along_y(x, k):
    return lax.ppermute(x, "ctx", [(y * NZ + z, (y + k) % NY * NZ + z) for y in range(NY) for z in range(NZ)])


def along_x(x, k):
    return lax.ppermute(x, "tp", [(2 * i + c, 2 * ((i + k) % NX) + c) for i in range(NX) for c in range(2)])


def at(x, i):
    return lax.dynamic_index_in_dim(x, i, 0, keepdims=False)


def regroup(x):
    pairs = []
    for y in range(NY):
        for z in range(NZ):
            pairs.append((y * NZ + z, (z % NY) * NZ + z // NY * NY + y))
    return lax.ppermute(x, "ctx", pairs)


def to_tiles(tile):
    pairs = []
    for y in range(NY):
        for z in range(NZ):
            for t in range(2 * NX):
                source = (y * NZ + z) * 2 * NX + t
                pairs.append((source, (y * NZ + t) * 2 * NX + 2 * (z % NY) + z // NY))
    return lax.ppermute(tile, ("ctx", "tp"), pairs)


def shards(
    queries,
    new_keys,
    new_values,
    store_keys,
    store_values,
    hit_blocks,
    hit_counts,
    new_lengths,
    out_weight,
):
    me = lax.axis_index("ctx")
    t = lax.axis_index("tp")
    y, z = me // NZ, me % NZ
    x, core = t // 2, t % 2

    weights = lax.all_gather(
        out_weight,
        "ctx",
        axis=0,
        tiled=False,
        axis_index_groups=[[yy * NZ + zz for zz in range(NZ)] for yy in range(NY)],
    )

    blocks = jnp.concatenate([store_keys, jnp.swapaxes(store_values, 1, 2)], axis=1).reshape(STORE * PAIR, HEAD)
    lists = jnp.stack([hit_blocks.reshape(-1), jnp.pad(hit_counts[0], (0, 128 - hit_counts.shape[1]))])
    store = jnp.concatenate([blocks, jnp.pad(lists, ((0, STATS - 2), (0, 0))).astype(BF16)], axis=0)
    store_l, store_r = along_y(store, 1), along_y(store, -1)
    middle = STORE // 2 * PAIR
    far = [along_y(store_l[:middle], 1), along_y(store_r[middle:], -1)]

    def listed(x):
        return x[-STATS : 2 - STATS].astype(jnp.int32)

    hits = [lists, listed(store_l), listed(store_r), listed(far[1])]

    half = ROWS // 2
    queries = regroup(queries)
    q_up = [queries]
    q_down = [queries]
    for _ in range(3):
        q_up.append(along_z(q_up[-1], -1))
        q_down.append(along_z(q_down[-1], 1))
    q_far = [along_z(q_down[3][:, :half], 1), along_z(q_up[3][:, half:], -1)]
    lengths = jnp.broadcast_to(new_lengths.astype(BF16)[:, None], (STATS, HEAD))
    new = regroup(jnp.concatenate([new_keys, new_values.T, lengths], axis=0))

    def number(*places):
        at_z = [(z + d) % NZ for d in places]
        return jnp.stack([(i % NY) * NZ + i // NY * NY + y for i in at_z]).astype(jnp.int32)

    run = functools.partial(attend, hits=hits, stores=[store, store_l, store_r], far=far)
    (opposite,) = run(number(4), qs=q_far, n_halves=2)
    got_l, got_r = along_z(opposite[:, :half], 1), along_z(opposite[:, half:], -1)
    for d in (3, 2, 1):
        both = run(number(d, -d), qs=[q_up[d], q_down[d]], n_halves=1)
        to_right, to_left = relay(d == 3, both, got_l, got_r)
        got_l, got_r = along_z(to_right, 1), along_z(to_left, -1)
    own = run(number(0), qs=[queries], n_halves=1, new_kv=(new,))
    head_out = finish(new, own, got_l, got_r)

    rows = jnp.concatenate([head_out, along_y(head_out, 1), along_y(head_out, 2), along_y(head_out, 3)], axis=0)
    pairs = weights.reshape(NX, 2, *out_weight.shape)
    other = lax.dynamic_index_in_dim(pairs, 1 - core, 1, keepdims=False)
    mine = lax.dynamic_index_in_dim(pairs, core, 1, keepdims=False)
    form = "rk,xkc->xrc"
    sent = jnp.einsum(form, rows, other, preferred_element_type=F32).astype(BF16)
    swapped = lax.ppermute(sent, "tp", [(i, i ^ 1) for i in range(2 * NX)])
    summed = lax.optimization_barrier(jnp.einsum(form, rows, mine, preferred_element_type=F32)) + swapped.astype(F32)
    thin = summed.astype(BF16)
    total = at(summed, x)
    for k in range(1, NX):
        total = total + along_x(at(thin, (x + k) % NX), k).astype(F32)
    tile = to_tiles(total.astype(BF16)).reshape(NY, TOK, out_weight.shape[1])
    turned = [tile[-k % NY] for k in range(NY)]
    ordered = lax.dynamic_slice_in_dim(jnp.stack(turned + turned), -y % NY, NY, 0)
    return ordered.reshape(NY * TOK, out_weight.shape[1])


def solution(mesh):
    return jax.shard_map(
        shards,
        mesh=mesh,
        in_specs=(
            P("ctx", "tp"),
            P("ctx", "tp"),
            P("ctx", "tp"),
            P("ctx", None, "tp"),
            P("ctx", None, "tp"),
            P("ctx", None, None),
            P("ctx", None),
            P("ctx"),
            P("tp", "ctx"),
        ),
        out_specs=P("tp", "ctx"),
        check_vma=False,
    )
```

```python
import functools

import jax
import jax.numpy as jnp
from jax import lax
from jax.experimental import pallas as pl
from jax.experimental.pallas import tpu as pltpu
from jax.sharding import PartitionSpec as P

HEAD = 128
BLOCK = 128
MOST = 4
TOK = 128
GROUP = 8
ROWS = GROUP * TOK
STORE = 16
NY = 4
NZ = 8
NX = 4
STATS = 16
PART = HEAD + STATS
PAIR = 2 * BLOCK
CHUNK = 8
TAILS = (2, 4, 8)
NEG = -1e30
SCALE2 = 1.4426950408889634 * HEAD**-0.5
VMEM_BYTES = 44 * 1024 * 1024
F32 = jnp.float32
BF16 = jnp.bfloat16


def heads_down(q):
    return jnp.concatenate([q[:, g * HEAD : (g + 1) * HEAD] for g in range(q.shape[1] // HEAD)], axis=0)


def scores(k, q):
    return lax.dot_general(k, q, (((1,), (1,)), ((), ())), preferred_element_type=F32)


def fold8(s):
    return jnp.max(s.reshape(s.shape[0] // 8, 8, s.shape[1]), axis=0)


def stat_rows(m, l):
    high = l.astype(BF16).astype(F32)
    row = lax.broadcasted_iota(jnp.int32, (STATS, m.shape[1]), 0)
    zero = jnp.zeros((STATS, m.shape[1]), F32)
    out = jnp.where(row == 0, m, zero)
    out = jnp.where(row == 1, high, out)
    return jnp.where(row == 2, l - high, out).astype(BF16)


def live_copies(seq, slot, hits, stores, kv, sems, act):
    pos = jnp.int32(0)
    for h, (hit, store) in enumerate(zip(hits, stores)):
        count = hit[1, seq]
        share = STORE // len(store)
        for j in range(MOST):
            block = hit[0, seq * MOST + j]
            for i, ref in enumerate(store):
                wanted = (j < count) & (block // share == i)

                @pl.when(wanted)
                def _(ref=ref, h=h, j=j, at=pos + j, row=block - i * share):
                    source = ref.at[pl.ds(pl.multiple_of(row * PAIR, PAIR), PAIR), :]
                    act(pltpu.make_async_copy(source, kv.at[slot, at], sems.at[slot, h * MOST + j]))

        pos = pos + count
    return pos


def parts_of(x):
    x = x.astype(F32)
    m = x[HEAD : HEAD + 1]
    l = x[HEAD + 1 : HEAD + 2] + x[HEAD + 2 : HEAD + 3]
    return x[0:HEAD], m, l


def merge(parts):
    top = functools.reduce(jnp.maximum, [m for _, m, _ in parts])
    weights = [jnp.exp2(m - top) for _, m, _ in parts]
    o = sum(w * o for w, (o, _, _) in zip(weights, parts))
    l = sum(w * l for w, (_, _, l) in zip(weights, parts))
    return o, top, l


def take(refs, n):
    return refs[:n], refs[n:]


def attend_kernel(n_seqs, n_halves, splits, with_new, with_prior, *refs):
    (seq_ref,), refs = take(refs, 1)
    hits, refs = take(refs, len(splits))
    q_refs, refs = take(refs, n_seqs * n_halves)
    stores = []
    for split in splits:
        store, refs = take(refs, split)
        stores.append(store)
    new, refs = take(refs, int(with_new))
    prior, refs = take(refs, int(with_prior))
    out, kv, q_scr, s_scr, m_scr, acc, sems = refs
    room = MOST * len(splits)
    chunk = min(CHUNK, room)
    copies = functools.partial(live_copies, hits=hits, stores=stores, kv=kv, sems=sems)
    for n in range(n_seqs):
        copies(seq_ref[n], n, act=lambda c: c.start())
    for n in range(n_seqs):
        mine = q_refs[n * n_halves : (n + 1) * n_halves]
        q_scr[n] = jnp.concatenate([heads_down(r[...]) for r in mine], axis=0)

    def one(n, carry):
        count = copies(seq_ref[n], n, act=lambda c: c.wait())
        full = count // chunk
        tail = count - full * chunk

        def blank(i, carry):
            kv[n, i, BLOCK:PAIR, :] = jnp.zeros((HEAD, BLOCK), BF16)
            return carry

        lax.fori_loop(count, jnp.minimum(count + chunk, room), blank, 0)

        def each(step):
            lax.fori_loop(0, full, lambda i, c: (step(i * chunk, chunk, False), c)[1], 0)
            low = 0
            for size in TAILS:
                if size <= chunk:

                    @pl.when((tail > low) & (tail <= size))
                    def _(size=size):
                        step(full * chunk, size, True)

                    low = size

        q = q_scr[n]
        m_scr[...] = jnp.full_like(m_scr, NEG)
        acc[...] = jnp.zeros_like(acc)

        def first(base, size, masked):
            k = kv[n, pl.ds(base, size)][:, 0:BLOCK, :].reshape(size * BLOCK, HEAD)
            s = scores(k, q)
            if masked:
                key = lax.broadcasted_iota(jnp.int32, s.shape, 0)
                s = jnp.where(key < tail * BLOCK, s, NEG)
            s_scr[pl.ds(base, size)] = s.reshape(size, BLOCK, ROWS)
            m_scr[...] = jnp.maximum(m_scr[...], fold8(s))

        each(first)
        if with_new:
            s = scores(new[0][0:BLOCK, :], q)
            key = lax.broadcasted_iota(jnp.int32, s.shape, 0)
            tok = lax.broadcasted_iota(jnp.int32, s.shape, 1) % TOK
            s = jnp.where(key <= tok, s, NEG)
            s_scr[room] = s
            m_scr[...] = jnp.maximum(m_scr[...], fold8(s))

        m = (jnp.max(m_scr[...], axis=0, keepdims=True) * SCALE2).astype(BF16).astype(F32)

        def weigh(s, v):
            p = jnp.exp2(s * SCALE2 - m).astype(BF16)
            v = jnp.concatenate([v, jnp.ones((STATS, v.shape[1]), BF16)], axis=0)
            acc[...] += jnp.dot(v, p, preferred_element_type=F32)

        def second(base, size, masked):
            s = s_scr[pl.ds(base, size)].reshape(size * BLOCK, ROWS)
            weigh(s, jnp.concatenate([kv[n, base + i][BLOCK:PAIR, :] for i in range(size)], axis=1))

        each(second)
        if with_new:
            weigh(s_scr[room], new[0][BLOCK:PAIR, :])
        o, l = acc[0:HEAD, :], acc[HEAD : HEAD + 1, :]
        if with_prior:
            o, m, l = merge([(o, m, l), parts_of(prior[0][n])])
        out[n, 0:HEAD, :] = o.astype(BF16)
        out[n, HEAD:PART, :] = stat_rows(m, l)
        return carry

    lax.fori_loop(0, n_seqs, one, 0)


def attend(seqs, hits, qs, n_halves, stores, new=(), prior=()):
    n_seqs = len(qs) // n_halves
    room = MOST * len(stores)
    smem = pl.BlockSpec(memory_space=pltpu.SMEM)
    vmem = pl.BlockSpec(memory_space=pltpu.VMEM)
    anywhere = pl.BlockSpec(memory_space=pl.ANY)
    splits = [len(store) for store in stores]
    flat = [piece for store in stores for piece in store]
    work = n_seqs * 2 * len(stores)
    return pl.pallas_call(
        functools.partial(attend_kernel, n_seqs, n_halves, splits, len(new) > 0, len(prior) > 0),
        out_shape=jax.ShapeDtypeStruct((n_seqs, PART, ROWS), BF16),
        in_specs=[smem] * (1 + len(hits)) + [vmem] * len(qs) + [anywhere] * len(flat) + [vmem] * len(new + prior),
        out_specs=vmem,
        scratch_shapes=[
            pltpu.VMEM((n_seqs, room, PAIR, HEAD), BF16),
            pltpu.VMEM((n_seqs, ROWS, HEAD), BF16),
            pltpu.VMEM((room + 1, BLOCK, ROWS), F32),
            pltpu.VMEM((8, ROWS), F32),
            pltpu.VMEM((PART, ROWS), F32),
            pltpu.SemaphoreType.DMA((n_seqs, room)),
        ],
        compiler_params=pltpu.CompilerParams(vmem_limit_bytes=VMEM_BYTES),
        cost_estimate=pl.CostEstimate(
            flops=work * 4 * BLOCK * ROWS * HEAD,
            bytes_accessed=5 * 2**20,
            transcendentals=work * BLOCK * ROWS,
        ),
    )(seqs, *hits, *qs, *flat, *new, *prior)


def relay_kernel(halves, own, got_a, got_b, out_a, out_b):
    half = ROWS // 2
    for n, (got, out) in enumerate(((got_a, out_a), (got_b, out_b))):
        cols = slice(0, ROWS)
        if halves:
            cols = slice(n * half, (n + 1) * half)
            rest = slice((1 - n) * half, (2 - n) * half)
            out[:, rest] = own[n, :, rest]
        o, m, l = merge([parts_of(own[n, :, cols]), parts_of(got[...])])
        out[0:HEAD, cols] = o.astype(BF16)
        out[HEAD:PART, cols] = stat_rows(m, l)


def relay(halves, own, got_a, got_b):
    vmem = pl.BlockSpec(memory_space=pltpu.VMEM)
    return pl.pallas_call(
        functools.partial(relay_kernel, halves),
        out_shape=[jax.ShapeDtypeStruct((PART, ROWS), BF16)] * 2,
        in_specs=[vmem] * 3,
        out_specs=[vmem] * 2,
        compiler_params=pltpu.CompilerParams(vmem_limit_bytes=VMEM_BYTES),
        cost_estimate=pl.CostEstimate(flops=8 * PART * ROWS, bytes_accessed=2 * 2**20, transcendentals=4 * ROWS),
    )(own, got_a, got_b)


def finish_kernel(new, own, left, right, out):
    o, _, l = merge([parts_of(own[0]), parts_of(left[...]), parts_of(right[...])])
    attended = o / l
    tok = lax.broadcasted_iota(jnp.int32, attended.shape, 1) % TOK
    length = new[PAIR : PAIR + STATS, :].astype(F32)[0:1, 0:1]
    attended = jnp.where(tok.astype(F32) < length, attended, 0.0)
    for g in range(GROUP):
        out[:, g * HEAD : (g + 1) * HEAD] = attended[:, g * TOK : (g + 1) * TOK].T.astype(BF16)


def finish(new, own, left, right):
    vmem = pl.BlockSpec(memory_space=pltpu.VMEM)
    return pl.pallas_call(
        finish_kernel,
        out_shape=jax.ShapeDtypeStruct((TOK, ROWS), BF16),
        in_specs=[vmem] * 4,
        out_specs=vmem,
        compiler_params=pltpu.CompilerParams(vmem_limit_bytes=VMEM_BYTES),
        cost_estimate=pl.CostEstimate(flops=8 * PART * ROWS, bytes_accessed=2**20, transcendentals=4 * ROWS),
    )(new, own, left, right)


def along_z(x, k):
    return lax.ppermute(x, "ctx", [(y * NZ + z, y * NZ + (z + k) % NZ) for y in range(NY) for z in range(NZ)])


def along_y(x, k):
    return lax.ppermute(x, "ctx", [(y * NZ + z, (y + k) % NY * NZ + z) for y in range(NY) for z in range(NZ)])


def along_x(x, k):
    return lax.ppermute(x, "tp", [(2 * i + c, 2 * ((i + k) % NX) + c) for i in range(NX) for c in range(2)])


def at(x, i):
    return lax.dynamic_index_in_dim(x, i, 0, keepdims=False)


def to_tiles(tile, y, z, t):
    got = []
    for r in range(NY):
        piece = at(tile, (y - r - z) % NY)
        pairs = []
        for yy in range(NY):
            for zz in range(NZ):
                for tt in range(2 * NX):
                    source = (yy * NZ + zz) * 2 * NX + tt
                    target = (yy * NZ + tt) * 2 * NX + 2 * ((r + zz) % NY) + zz // 4
                    pairs.append((source, target))
        got.append(lax.ppermute(piece, ("ctx", "tp"), pairs))
    turned = [got[(-j) % NY] for j in range(NY)]
    both = jnp.concatenate(turned + turned, axis=0)
    start = (-(t // 2)) % NY
    return lax.dynamic_slice_in_dim(both, start * TOK, NY * TOK, 0)


def shards(
    queries,
    new_keys,
    new_values,
    store_keys,
    store_values,
    hit_blocks,
    hit_counts,
    new_lengths,
    out_weight,
):
    me = lax.axis_index("ctx")
    t = lax.axis_index("tp")
    y, z = me // NZ, me % NZ
    x, core = t // 2, t % 2

    blocks = jnp.concatenate([store_keys, jnp.swapaxes(store_values, 1, 2)], axis=1).reshape(STORE * PAIR, HEAD)
    lists = jnp.stack([hit_blocks.reshape(-1), jnp.pad(hit_counts[0], (0, 128 - hit_counts.shape[1]))])
    store = jnp.concatenate([blocks, jnp.pad(lists, ((0, STATS - 2), (0, 0))).astype(BF16)], axis=0)
    store_l, store_r = along_y(store, 1), along_y(store, -1)
    middle = STORE // 2 * PAIR
    far = [along_y(store_l[:middle], 1), along_y(store_r[middle:], -1)]

    def listed(x):
        return x[-STATS : 2 - STATS].astype(jnp.int32)

    hits = [lists, listed(store_l), listed(store_r), listed(far[1])]

    half = ROWS // 2
    q_up = [queries]
    q_down = [queries]
    for step in range(3):
        up, down = q_up[-1], q_down[-1]
        if step == 2:
            up, down, _, _ = lax.optimization_barrier((up, down, store_l, store_r))
        q_up.append(along_z(up, -1))
        q_down.append(along_z(down, 1))
    q_far = [along_z(q_down[3][:, :half], 1), along_z(q_up[3][:, half:], -1)]
    lengths = jnp.broadcast_to(new_lengths.astype(BF16)[:, None], (STATS, HEAD))
    new = jnp.concatenate([new_keys, new_values.T, lengths], axis=0)

    def number(*places):
        return jnp.stack([y * NZ + (z + d) % NZ for d in places]).astype(jnp.int32)

    near = functools.partial(attend, hits=hits[:3], stores=[(store,), (store_l,), (store_r,)])
    first = {d: near(number(d, -d), qs=[q_up[d], q_down[d]], n_halves=1) for d in (1, 2, 3)}
    first[4] = near(number(4), qs=q_far, n_halves=2)
    first[0] = near(number(0), qs=[queries], n_halves=1, new=(new,))
    far, hit_far, first[2], first[3], first[4], out_weight = lax.optimization_barrier(
        (far, hits[3], first[2], first[3], first[4], out_weight)
    )
    last = functools.partial(attend, hits=[hit_far], stores=[far])

    weights = lax.all_gather(
        out_weight,
        "ctx",
        axis=0,
        tiled=False,
        axis_index_groups=[[yy * NZ + zz for zz in range(NZ)] for yy in range(NY)],
    )

    (opposite,) = last(number(4), qs=q_far, n_halves=2, prior=(first[4],))
    got_l, got_r = along_z(opposite[:, :half], 1), along_z(opposite[:, half:], -1)
    for d in (3, 2, 1):
        both = last(number(d, -d), qs=[q_up[d], q_down[d]], n_halves=1, prior=(first[d],))
        to_right, to_left = relay(d == 3, both, got_l, got_r)
        got_l, got_r = along_z(to_right, 1), along_z(to_left, -1)
    own = last(number(0), qs=[queries], n_halves=1, prior=(first[0],))
    head_out = finish(new, own, got_l, got_r)

    rows = jnp.concatenate([head_out, along_y(head_out, 1), along_y(head_out, 2), along_y(head_out, 3)], axis=0)
    pairs = weights.reshape(NX, 2, *out_weight.shape)
    other = lax.dynamic_index_in_dim(pairs, 1 - core, 1, keepdims=False)
    mine = lax.dynamic_index_in_dim(pairs, core, 1, keepdims=False)
    form = "rk,xkc->xrc"
    sent = jnp.einsum(form, rows, other, preferred_element_type=F32).astype(BF16)
    swapped = lax.ppermute(sent, "tp", [(i, i ^ 1) for i in range(2 * NX)])
    summed = lax.optimization_barrier(jnp.einsum(form, rows, mine, preferred_element_type=F32)) + swapped.astype(F32)
    thin = summed.astype(BF16)
    total = at(summed, x)
    for k in range(1, NX):
        total = total + along_x(at(thin, (x + k) % NX), k).astype(F32)
    tile = total.astype(BF16).reshape(NY, TOK, out_weight.shape[1])
    return to_tiles(tile, y, z, t)


def solution(mesh):
    return jax.shard_map(
        shards,
        mesh=mesh,
        in_specs=(
            P("ctx", "tp"),
            P("ctx", "tp"),
            P("ctx", "tp"),
            P("ctx", None, "tp"),
            P("ctx", None, "tp"),
            P("ctx", None, None),
            P("ctx", None),
            P("ctx"),
            P("tp", "ctx"),
        ),
        out_specs=P("tp", "ctx"),
        check_vma=False,
    )
```

```python
import functools

import jax
import jax.numpy as jnp
from jax import lax
from jax.experimental import pallas as pl
from jax.experimental.pallas import tpu as pltpu
from jax.sharding import PartitionSpec as P

HEAD = 128
BLOCK = 128
MOST = 4
TOK = 128
GROUP = 8
ROWS = GROUP * TOK
STORE = 16
NY = 4
NZ = 8
NX = 4
STATS = 16
PART = HEAD + STATS
PAIR = 2 * BLOCK
CHUNK = 8
TAILS = (2, 4, 8)
NEG = -1e30
SCALE2 = 1.4426950408889634 * HEAD**-0.5
VMEM_BYTES = 24 * 1024 * 1024
F32 = jnp.float32
BF16 = jnp.bfloat16


def heads_down(q):
    return jnp.concatenate([q[:, g * HEAD : (g + 1) * HEAD] for g in range(q.shape[1] // HEAD)], axis=0)


def scores(k, q):
    return lax.dot_general(k, q, (((1,), (1,)), ((), ())), preferred_element_type=F32)


def fold8(s):
    return jnp.max(s.reshape(s.shape[0] // 8, 8, s.shape[1]), axis=0)


def stat_rows(m, l):
    high = l.astype(BF16).astype(F32)
    row = lax.broadcasted_iota(jnp.int32, (STATS, m.shape[1]), 0)
    zero = jnp.zeros((STATS, m.shape[1]), F32)
    out = jnp.where(row == 0, m, zero)
    out = jnp.where(row == 1, high, out)
    return jnp.where(row == 2, l - high, out).astype(BF16)


def live_copies(seq, slot, hits, stores, kv, sems, act):
    pos = jnp.int32(0)
    for h, (hit, store) in enumerate(zip(hits, stores)):
        count = hit[1, seq]
        share = STORE // len(store)
        for j in range(MOST):
            block = hit[0, seq * MOST + j]
            for i, ref in enumerate(store):
                wanted = (j < count) & (block // share == i)

                @pl.when(wanted)
                def _(ref=ref, h=h, j=j, at=pos + j, row=block - i * share):
                    source = ref.at[pl.ds(pl.multiple_of(row * PAIR, PAIR), PAIR), :]
                    act(pltpu.make_async_copy(source, kv.at[slot, at], sems.at[slot, h * MOST + j]))

        pos = pos + count
    return pos


def parts_of(x):
    x = x.astype(F32)
    m = x[HEAD : HEAD + 1]
    l = x[HEAD + 1 : HEAD + 2] + x[HEAD + 2 : HEAD + 3]
    return x[0:HEAD], m, l


def merge(parts):
    top = functools.reduce(jnp.maximum, [m for _, m, _ in parts])
    weights = [jnp.exp2(m - top) for _, m, _ in parts]
    o = sum(w * o for w, (o, _, _) in zip(weights, parts))
    l = sum(w * l for w, (_, _, l) in zip(weights, parts))
    return o, top, l


def take(refs, n):
    return refs[:n], refs[n:]


def attend_kernel(n_seqs, n_halves, splits, with_new, with_prior, *refs):
    (seq_ref,), refs = take(refs, 1)
    hits, refs = take(refs, len(splits))
    q_refs, refs = take(refs, n_seqs * n_halves)
    stores = []
    for split in splits:
        store, refs = take(refs, split)
        stores.append(store)
    new, refs = take(refs, int(with_new))
    prior, refs = take(refs, int(with_prior))
    out, kv, q_scr, s_scr, m_scr, acc, sems = refs
    room = MOST * len(splits)
    chunk = min(CHUNK, room)
    copies = functools.partial(live_copies, hits=hits, stores=stores, kv=kv, sems=sems)
    for n in range(n_seqs):
        copies(seq_ref[n], n, act=lambda c: c.start())
    for n in range(n_seqs):
        mine = q_refs[n * n_halves : (n + 1) * n_halves]
        q_scr[n] = jnp.concatenate([heads_down(r[...]) for r in mine], axis=0)

    def one(n, carry):
        count = copies(seq_ref[n], n, act=lambda c: c.wait())
        full = count // chunk
        tail = count - full * chunk

        def blank(i, carry):
            kv[n, i, BLOCK:PAIR, :] = jnp.zeros((HEAD, BLOCK), BF16)
            return carry

        lax.fori_loop(count, jnp.minimum(count + chunk, room), blank, 0)

        def each(step):
            lax.fori_loop(0, full, lambda i, c: (step(i * chunk, chunk, False), c)[1], 0)
            low = 0
            for size in TAILS:
                if size <= chunk:

                    @pl.when((tail > low) & (tail <= size))
                    def _(size=size):
                        step(full * chunk, size, True)

                    low = size

        q = q_scr[n]
        m_scr[...] = jnp.full_like(m_scr, NEG)
        acc[...] = jnp.zeros_like(acc)

        def first(base, size, masked):
            k = kv[n, pl.ds(base, size)][:, 0:BLOCK, :].reshape(size * BLOCK, HEAD)
            s = scores(k, q)
            if masked:
                key = lax.broadcasted_iota(jnp.int32, s.shape, 0)
                s = jnp.where(key < tail * BLOCK, s, NEG)
            s_scr[pl.ds(base, size)] = s.reshape(size, BLOCK, ROWS)
            m_scr[...] = jnp.maximum(m_scr[...], fold8(s))

        each(first)
        if with_new:
            s = scores(new[0][0:BLOCK, :], q)
            key = lax.broadcasted_iota(jnp.int32, s.shape, 0)
            tok = lax.broadcasted_iota(jnp.int32, s.shape, 1) % TOK
            s = jnp.where(key <= tok, s, NEG)
            s_scr[room] = s
            m_scr[...] = jnp.maximum(m_scr[...], fold8(s))

        m = (jnp.max(m_scr[...], axis=0, keepdims=True) * SCALE2).astype(BF16).astype(F32)

        def weigh(s, v):
            p = jnp.exp2(s * SCALE2 - m).astype(BF16)
            v = jnp.concatenate([v, jnp.ones((STATS, v.shape[1]), BF16)], axis=0)
            acc[...] += jnp.dot(v, p, preferred_element_type=F32)

        def second(base, size, masked):
            s = s_scr[pl.ds(base, size)].reshape(size * BLOCK, ROWS)
            weigh(s, jnp.concatenate([kv[n, base + i][BLOCK:PAIR, :] for i in range(size)], axis=1))

        each(second)
        if with_new:
            weigh(s_scr[room], new[0][BLOCK:PAIR, :])
        o, l = acc[0:HEAD, :], acc[HEAD : HEAD + 1, :]
        if with_prior:
            o, m, l = merge([(o, m, l), parts_of(prior[0][n])])
        out[n, 0:HEAD, :] = o.astype(BF16)
        out[n, HEAD:PART, :] = stat_rows(m, l)
        return carry

    lax.fori_loop(0, n_seqs, one, 0)


def attend(seqs, hits, qs, n_halves, stores, new=(), prior=()):
    n_seqs = len(qs) // n_halves
    room = MOST * len(stores)
    smem = pl.BlockSpec(memory_space=pltpu.SMEM)
    vmem = pl.BlockSpec(memory_space=pltpu.VMEM)
    anywhere = pl.BlockSpec(memory_space=pl.ANY)
    splits = [len(store) for store in stores]
    flat = [piece for store in stores for piece in store]
    work = n_seqs * 2 * len(stores)
    return pl.pallas_call(
        functools.partial(attend_kernel, n_seqs, n_halves, splits, len(new) > 0, len(prior) > 0),
        out_shape=jax.ShapeDtypeStruct((n_seqs, PART, ROWS), BF16),
        in_specs=[smem] * (1 + len(hits)) + [vmem] * len(qs) + [anywhere] * len(flat) + [vmem] * len(new + prior),
        out_specs=vmem,
        scratch_shapes=[
            pltpu.VMEM((n_seqs, room, PAIR, HEAD), BF16),
            pltpu.VMEM((n_seqs, ROWS, HEAD), BF16),
            pltpu.VMEM((room + 1, BLOCK, ROWS), F32),
            pltpu.VMEM((8, ROWS), F32),
            pltpu.VMEM((PART, ROWS), F32),
            pltpu.SemaphoreType.DMA((n_seqs, room)),
        ],
        compiler_params=pltpu.CompilerParams(vmem_limit_bytes=VMEM_BYTES),
        cost_estimate=pl.CostEstimate(
            flops=work * 4 * BLOCK * ROWS * HEAD,
            bytes_accessed=5 * 2**20,
            transcendentals=work * BLOCK * ROWS,
        ),
    )(seqs, *hits, *qs, *flat, *new, *prior)


def relay_kernel(halves, own, got_a, got_b, out_a, out_b):
    half = ROWS // 2
    for n, (got, out) in enumerate(((got_a, out_a), (got_b, out_b))):
        cols = slice(0, ROWS)
        if halves:
            cols = slice(n * half, (n + 1) * half)
            rest = slice((1 - n) * half, (2 - n) * half)
            out[:, rest] = own[n, :, rest]
        o, m, l = merge([parts_of(own[n, :, cols]), parts_of(got[...])])
        out[0:HEAD, cols] = o.astype(BF16)
        out[HEAD:PART, cols] = stat_rows(m, l)


def relay(halves, own, got_a, got_b):
    vmem = pl.BlockSpec(memory_space=pltpu.VMEM)
    return pl.pallas_call(
        functools.partial(relay_kernel, halves),
        out_shape=[jax.ShapeDtypeStruct((PART, ROWS), BF16)] * 2,
        in_specs=[vmem] * 3,
        out_specs=[vmem] * 2,
        compiler_params=pltpu.CompilerParams(vmem_limit_bytes=VMEM_BYTES),
        cost_estimate=pl.CostEstimate(flops=8 * PART * ROWS, bytes_accessed=2 * 2**20, transcendentals=4 * ROWS),
    )(own, got_a, got_b)


def finish_kernel(new, own, left, right, out):
    o, _, l = merge([parts_of(own[0]), parts_of(left[...]), parts_of(right[...])])
    attended = o / l
    tok = lax.broadcasted_iota(jnp.int32, attended.shape, 1) % TOK
    length = new[PAIR : PAIR + STATS, :].astype(F32)[0:1, 0:1]
    attended = jnp.where(tok.astype(F32) < length, attended, 0.0)
    for g in range(GROUP):
        out[:, g * HEAD : (g + 1) * HEAD] = attended[:, g * TOK : (g + 1) * TOK].T.astype(BF16)


def finish(new, own, left, right):
    vmem = pl.BlockSpec(memory_space=pltpu.VMEM)
    return pl.pallas_call(
        finish_kernel,
        out_shape=jax.ShapeDtypeStruct((TOK, ROWS), BF16),
        in_specs=[vmem] * 4,
        out_specs=vmem,
        compiler_params=pltpu.CompilerParams(vmem_limit_bytes=VMEM_BYTES),
        cost_estimate=pl.CostEstimate(flops=8 * PART * ROWS, bytes_accessed=2**20, transcendentals=4 * ROWS),
    )(new, own, left, right)


def along_z(x, k):
    return lax.ppermute(x, "ctx", [(y * NZ + z, y * NZ + (z + k) % NZ) for y in range(NY) for z in range(NZ)])


def along_y(x, k):
    return lax.ppermute(x, "ctx", [(y * NZ + z, (y + k) % NY * NZ + z) for y in range(NY) for z in range(NZ)])


def along_x(x, k):
    return lax.ppermute(x, "tp", [(2 * i + c, 2 * ((i + k) % NX) + c) for i in range(NX) for c in range(2)])


def at(x, i):
    return lax.dynamic_index_in_dim(x, i, 0, keepdims=False)


def to_tiles(tile, y, z, t):
    got = []
    for r in range(NY):
        piece = at(tile, (y - r - z) % NY)
        pairs = []
        for yy in range(NY):
            for zz in range(NZ):
                for tt in range(2 * NX):
                    source = (yy * NZ + zz) * 2 * NX + tt
                    target = (yy * NZ + tt) * 2 * NX + 2 * ((r + zz) % NY) + zz // 4
                    pairs.append((source, target))
        got.append(lax.ppermute(piece, ("ctx", "tp"), pairs))
    turned = [got[(-j) % NY] for j in range(NY)]
    both = jnp.concatenate(turned + turned, axis=0)
    start = (-(t // 2)) % NY
    return lax.dynamic_slice_in_dim(both, start * TOK, NY * TOK, 0)


def shards(
    queries,
    new_keys,
    new_values,
    store_keys,
    store_values,
    hit_blocks,
    hit_counts,
    new_lengths,
    out_weight,
):
    me = lax.axis_index("ctx")
    t = lax.axis_index("tp")
    y, z = me // NZ, me % NZ
    x, core = t // 2, t % 2

    weights = lax.all_gather(
        out_weight,
        "ctx",
        axis=0,
        tiled=False,
        axis_index_groups=[[yy * NZ + zz for zz in range(NZ)] for yy in range(NY)],
    )

    blocks = jnp.concatenate([store_keys, jnp.swapaxes(store_values, 1, 2)], axis=1).reshape(STORE * PAIR, HEAD)
    lists = jnp.stack([hit_blocks.reshape(-1), jnp.pad(hit_counts[0], (0, 128 - hit_counts.shape[1]))])
    store = jnp.concatenate([blocks, jnp.pad(lists, ((0, STATS - 2), (0, 0))).astype(BF16)], axis=0)
    store_l, store_r = along_y(store, 1), along_y(store, -1)
    middle = STORE // 2 * PAIR
    far = [along_y(store_l[:middle], 1), along_y(store_r[middle:], -1)]

    def listed(x):
        return x[-STATS : 2 - STATS].astype(jnp.int32)

    hits = [lists, listed(store_l), listed(store_r), listed(far[1])]

    half = ROWS // 2
    q_up = [queries]
    q_down = [queries]
    for step in range(3):
        up, down = q_up[-1], q_down[-1]
        if step == 2:
            up, down, _, _ = lax.optimization_barrier((up, down, store_l, store_r))
        q_up.append(along_z(up, -1))
        q_down.append(along_z(down, 1))
    q_far = [along_z(q_down[3][:, :half], 1), along_z(q_up[3][:, half:], -1)]
    lengths = jnp.broadcast_to(new_lengths.astype(BF16)[:, None], (STATS, HEAD))
    new = jnp.concatenate([new_keys, new_values.T, lengths], axis=0)

    def number(*places):
        return jnp.stack([y * NZ + (z + d) % NZ for d in places]).astype(jnp.int32)

    run = functools.partial(attend, hits=hits, stores=[(store,), (store_l,), (store_r,), far])
    (opposite,) = run(number(4), qs=q_far, n_halves=2)
    got_l, got_r = along_z(opposite[:, :half], 1), along_z(opposite[:, half:], -1)
    for d in (3, 2, 1):
        both = run(number(d, -d), qs=[q_up[d], q_down[d]], n_halves=1)
        to_right, to_left = relay(d == 3, both, got_l, got_r)
        got_l, got_r = along_z(to_right, 1), along_z(to_left, -1)
    own = run(number(0), qs=[queries], n_halves=1, new=(new,))
    head_out = finish(new, own, got_l, got_r)

    rows = jnp.concatenate([head_out, along_y(head_out, 1), along_y(head_out, 2), along_y(head_out, 3)], axis=0)
    pairs = weights.reshape(NX, 2, *out_weight.shape)
    other = lax.dynamic_index_in_dim(pairs, 1 - core, 1, keepdims=False)
    mine = lax.dynamic_index_in_dim(pairs, core, 1, keepdims=False)
    form = "rk,xkc->xrc"
    sent = jnp.einsum(form, rows, other, preferred_element_type=F32).astype(BF16)
    swapped = lax.ppermute(sent, "tp", [(i, i ^ 1) for i in range(2 * NX)])
    summed = lax.optimization_barrier(jnp.einsum(form, rows, mine, preferred_element_type=F32)) + swapped.astype(F32)
    thin = summed.astype(BF16)
    total = at(summed, x)
    for k in range(1, NX):
        total = total + along_x(at(thin, (x + k) % NX), k).astype(F32)
    tile = total.astype(BF16).reshape(NY, TOK, out_weight.shape[1])
    return to_tiles(tile, y, z, t)


def solution(mesh):
    return jax.shard_map(
        shards,
        mesh=mesh,
        in_specs=(
            P("ctx", "tp"),
            P("ctx", "tp"),
            P("ctx", "tp"),
            P("ctx", None, "tp"),
            P("ctx", None, "tp"),
            P("ctx", None, None),
            P("ctx", None),
            P("ctx"),
            P("tp", "ctx"),
        ),
        out_specs=P("tp", "ctx"),
        check_vma=False,
    )
```

```python
import functools

import jax
import jax.numpy as jnp
from jax import lax
from jax.experimental import pallas as pl
from jax.experimental.pallas import tpu as pltpu
from jax.sharding import PartitionSpec as P

HEAD = 128
BLOCK = 128
MOST = 4
TOK = 128
GROUP = 8
ROWS = GROUP * TOK
STORE = 16
NY = 4
NZ = 8
NX = 4
STATS = 16
PART = HEAD + STATS
PAIR = 2 * BLOCK
CHUNK = 8
TAILS = (2, 4, 8)
ROOM = STORE + CHUNK
NEG = -1e30
SCALE2 = 1.4426950408889634 * HEAD**-0.5
VMEM_BYTES = 24 * 1024 * 1024
F32 = jnp.float32
BF16 = jnp.bfloat16


def heads_down(q):
    return jnp.concatenate([q[:, g * HEAD : (g + 1) * HEAD] for g in range(q.shape[1] // HEAD)], axis=0)


def scores(k, q):
    return lax.dot_general(k, q, (((1,), (1,)), ((), ())), preferred_element_type=F32)


def fold8(s):
    return jnp.max(s.reshape(s.shape[0] // 8, 8, s.shape[1]), axis=0)


def stat_rows(m, l):
    high = l.astype(BF16).astype(F32)
    row = lax.broadcasted_iota(jnp.int32, (STATS, m.shape[1]), 0)
    zero = jnp.zeros((STATS, m.shape[1]), F32)
    out = jnp.where(row == 0, m, zero)
    out = jnp.where(row == 1, high, out)
    return jnp.where(row == 2, l - high, out).astype(BF16)


def parts_of(x):
    x = x.astype(F32)
    m = x[HEAD : HEAD + 1]
    l = x[HEAD + 1 : HEAD + 2] + x[HEAD + 2 : HEAD + 3]
    return x[0:HEAD], m, l


def merge(parts):
    top = functools.reduce(jnp.maximum, [m for _, m, _ in parts])
    weights = [jnp.exp2(m - top) for _, m, _ in parts]
    o = sum(w * o for w, (o, _, _) in zip(weights, parts))
    l = sum(w * l for w, (_, _, l) in zip(weights, parts))
    return o, top, l


def take(refs, n):
    return refs[:n], refs[n:]


def attend_kernel(n_seqs, n_halves, with_new, *refs):
    (seq_ref,), refs = take(refs, 1)
    hits, refs = take(refs, NY)
    q_refs, refs = take(refs, n_seqs * n_halves)
    stores, refs = take(refs, NY + 1)
    new, refs = take(refs, int(with_new))
    out, kv, q_raw, q_scr, s_scr, m_scr, acc, places, sems, q_sems = refs

    row = 0
    loads = []
    for i, ref in enumerate(stores):
        size = STORE * PAIR // (1 if i < NY - 1 else 2)
        loads.append(pltpu.make_async_copy(ref.at[pl.ds(0, size), :], kv.at[pl.ds(row, size), :], sems.at[i]))
        row += size
    q_loads = []
    width = ROWS // n_halves
    for i, ref in enumerate(q_refs):
        n, h = i // n_halves, i % n_halves
        q_loads.append(pltpu.make_async_copy(ref, q_raw.at[n, h], q_sems.at[i]))
    for load in q_loads + loads:
        load.start()

    counts = []
    for n in range(n_seqs):
        for i in range(ROOM):
            places[n, i] = 0
        pos = jnp.int32(0)
        seq = seq_ref[n]
        for h, hit in enumerate(hits):
            count = hit[1, seq]
            for j in range(MOST):
                places[n, pos] = h * STORE + hit[0, seq * MOST + j]
                pos = pos + (j < count).astype(jnp.int32)
        places[n, ROOM] = pos

    for load in q_loads:
        load.wait()
    for n in range(n_seqs):
        for g in range(GROUP):
            h, at = divmod(g * HEAD, width)
            q_scr[n, g * TOK : (g + 1) * TOK, :] = q_raw[n, h, :, at : at + HEAD]
    for load in loads:
        load.wait()

    def one(n, carry):
        count = places[n, ROOM]
        full = count // CHUNK
        tail = count - full * CHUNK

        def each(step):
            lax.fori_loop(0, full, lambda i, c: (step(i * CHUNK, CHUNK, False), c)[1], 0)
            low = 0
            for size in TAILS:

                @pl.when((tail > low) & (tail <= size))
                def _(size=size):
                    step(full * CHUNK, size, True)

                low = size

        def rows_of(base, size, shift):
            first = [pl.multiple_of(places[n, base + i] * PAIR + shift, BLOCK) for i in range(size)]
            return [kv[pl.ds(at, BLOCK), :] for at in first]

        q = q_scr[n]
        m_scr[...] = jnp.full_like(m_scr, NEG)
        acc[...] = jnp.zeros_like(acc)

        def first(base, size, masked):
            s = scores(jnp.concatenate(rows_of(base, size, 0), axis=0), q)
            if masked:
                key = lax.broadcasted_iota(jnp.int32, s.shape, 0)
                s = jnp.where(key < tail * BLOCK, s, NEG)
            s_scr[pl.ds(base, size)] = s.reshape(size, BLOCK, ROWS)
            m_scr[...] = jnp.maximum(m_scr[...], fold8(s))

        each(first)
        if with_new:
            s = scores(new[0][0:BLOCK, :], q)
            key = lax.broadcasted_iota(jnp.int32, s.shape, 0)
            tok = lax.broadcasted_iota(jnp.int32, s.shape, 1) % TOK
            s = jnp.where(key <= tok, s, NEG)
            s_scr[STORE] = s
            m_scr[...] = jnp.maximum(m_scr[...], fold8(s))

        m = (jnp.max(m_scr[...], axis=0, keepdims=True) * SCALE2).astype(BF16).astype(F32)

        def weigh(s, v):
            p = jnp.exp2(s * SCALE2 - m).astype(BF16)
            v = jnp.concatenate([v, jnp.ones((STATS, v.shape[1]), BF16)], axis=0)
            acc[...] += jnp.dot(v, p, preferred_element_type=F32)

        def second(base, size, masked):
            s = s_scr[pl.ds(base, size)].reshape(size * BLOCK, ROWS)
            weigh(s, jnp.concatenate(rows_of(base, size, BLOCK), axis=1))

        each(second)
        if with_new:
            weigh(s_scr[STORE], new[0][BLOCK:PAIR, :])
        out[n, 0:HEAD, :] = acc[0:HEAD, :].astype(BF16)
        out[n, HEAD:PART, :] = stat_rows(m, acc[HEAD : HEAD + 1, :])
        return carry

    lax.fori_loop(0, n_seqs, one, 0)


def attend(seqs, hits, qs, n_halves, stores, new=()):
    n_seqs = len(qs) // n_halves
    smem = pl.BlockSpec(memory_space=pltpu.SMEM)
    vmem = pl.BlockSpec(memory_space=pltpu.VMEM)
    anywhere = pl.BlockSpec(memory_space=pl.ANY)
    work = n_seqs * 8
    return pl.pallas_call(
        functools.partial(attend_kernel, n_seqs, n_halves, len(new) > 0),
        out_shape=jax.ShapeDtypeStruct((n_seqs, PART, ROWS), BF16),
        in_specs=[smem] * (1 + NY) + [anywhere] * (len(qs) + len(stores)) + [vmem] * len(new),
        out_specs=vmem,
        scratch_shapes=[
            pltpu.VMEM((NY * STORE * PAIR, HEAD), BF16),
            pltpu.VMEM((n_seqs, n_halves, TOK, ROWS // n_halves), BF16),
            pltpu.VMEM((n_seqs, ROWS, HEAD), BF16),
            pltpu.VMEM((STORE + 1, BLOCK, ROWS), F32),
            pltpu.VMEM((8, ROWS), F32),
            pltpu.VMEM((PART, ROWS), F32),
            pltpu.SMEM((n_seqs, ROOM + 1), jnp.int32),
            pltpu.SemaphoreType.DMA((NY + 1,)),
            pltpu.SemaphoreType.DMA((len(qs),)),
        ],
        compiler_params=pltpu.CompilerParams(vmem_limit_bytes=VMEM_BYTES),
        cost_estimate=pl.CostEstimate(
            flops=work * 4 * BLOCK * ROWS * HEAD,
            bytes_accessed=5 * 2**20,
            transcendentals=work * BLOCK * ROWS,
        ),
    )(seqs, *hits, *qs, *stores, *new)


def relay_kernel(halves, own, got_a, got_b, out_a, out_b):
    half = ROWS // 2
    for n, (got, out) in enumerate(((got_a, out_a), (got_b, out_b))):
        cols = slice(0, ROWS)
        if halves:
            cols = slice(n * half, (n + 1) * half)
            rest = slice((1 - n) * half, (2 - n) * half)
            out[:, rest] = own[n, :, rest]
        o, m, l = merge([parts_of(own[n, :, cols]), parts_of(got[...])])
        out[0:HEAD, cols] = o.astype(BF16)
        out[HEAD:PART, cols] = stat_rows(m, l)


def relay(halves, own, got_a, got_b):
    vmem = pl.BlockSpec(memory_space=pltpu.VMEM)
    return pl.pallas_call(
        functools.partial(relay_kernel, halves),
        out_shape=[jax.ShapeDtypeStruct((PART, ROWS), BF16)] * 2,
        in_specs=[vmem] * 3,
        out_specs=[vmem] * 2,
        compiler_params=pltpu.CompilerParams(vmem_limit_bytes=VMEM_BYTES),
        cost_estimate=pl.CostEstimate(flops=8 * PART * ROWS, bytes_accessed=2 * 2**20, transcendentals=4 * ROWS),
    )(own, got_a, got_b)


def finish_kernel(new, own, left, right, out):
    o, _, l = merge([parts_of(own[0]), parts_of(left[...]), parts_of(right[...])])
    attended = o / l
    tok = lax.broadcasted_iota(jnp.int32, attended.shape, 1) % TOK
    length = new[PAIR : PAIR + STATS, :].astype(F32)[0:1, 0:1]
    attended = jnp.where(tok.astype(F32) < length, attended, 0.0)
    for g in range(GROUP):
        out[:, g * HEAD : (g + 1) * HEAD] = attended[:, g * TOK : (g + 1) * TOK].T.astype(BF16)


def finish(new, own, left, right):
    vmem = pl.BlockSpec(memory_space=pltpu.VMEM)
    return pl.pallas_call(
        finish_kernel,
        out_shape=jax.ShapeDtypeStruct((TOK, ROWS), BF16),
        in_specs=[vmem] * 4,
        out_specs=vmem,
        compiler_params=pltpu.CompilerParams(vmem_limit_bytes=VMEM_BYTES),
        cost_estimate=pl.CostEstimate(flops=8 * PART * ROWS, bytes_accessed=2**20, transcendentals=4 * ROWS),
    )(new, own, left, right)


def along_z(x, k):
    return lax.ppermute(x, "ctx", [(y * NZ + z, y * NZ + (z + k) % NZ) for y in range(NY) for z in range(NZ)])


def along_y(x, k):
    return lax.ppermute(x, "ctx", [(y * NZ + z, (y + k) % NY * NZ + z) for y in range(NY) for z in range(NZ)])


def along_x(x, k):
    return lax.ppermute(x, "tp", [(2 * i + c, 2 * ((i + k) % NX) + c) for i in range(NX) for c in range(2)])


def at(x, i):
    return lax.dynamic_index_in_dim(x, i, 0, keepdims=False)


def to_tiles(tile, y, z, t):
    got = []
    for r in range(NY):
        piece = at(tile, (y - r - z) % NY)
        pairs = []
        for yy in range(NY):
            for zz in range(NZ):
                for tt in range(2 * NX):
                    source = (yy * NZ + zz) * 2 * NX + tt
                    target = (yy * NZ + tt) * 2 * NX + 2 * ((r + zz) % NY) + zz // 4
                    pairs.append((source, target))
        got.append(lax.ppermute(piece, ("ctx", "tp"), pairs))
    turned = [got[(-j) % NY] for j in range(NY)]
    both = jnp.concatenate(turned + turned, axis=0)
    start = (-(t // 2)) % NY
    return lax.dynamic_slice_in_dim(both, start * TOK, NY * TOK, 0)


def shards(
    queries,
    new_keys,
    new_values,
    store_keys,
    store_values,
    hit_blocks,
    hit_counts,
    new_lengths,
    out_weight,
):
    me = lax.axis_index("ctx")
    t = lax.axis_index("tp")
    y, z = me // NZ, me % NZ
    x, core = t // 2, t % 2

    weights = lax.all_gather(
        out_weight,
        "ctx",
        axis=0,
        tiled=False,
        axis_index_groups=[[yy * NZ + zz for zz in range(NZ)] for yy in range(NY)],
    )

    blocks = jnp.concatenate([store_keys, jnp.swapaxes(store_values, 1, 2)], axis=1).reshape(STORE * PAIR, HEAD)
    lists = jnp.stack([hit_blocks.reshape(-1), jnp.pad(hit_counts[0], (0, 128 - hit_counts.shape[1]))])
    store = jnp.concatenate([blocks, jnp.pad(lists, ((0, STATS - 2), (0, 0))).astype(BF16)], axis=0)
    store_l, store_r = along_y(store, 1), along_y(store, -1)
    middle = STORE // 2 * PAIR
    second = [store_l[:middle], store_r[middle:]]
    far = [along_y(second[0], 1), along_y(second[1], -1)]

    def listed(x):
        return x[-STATS : 2 - STATS].astype(jnp.int32)

    hits = [lists, listed(store_l), listed(store_r), listed(far[1])]

    half = ROWS // 2
    q_up = [queries]
    q_down = [queries]
    for _ in range(3):
        q_up.append(along_z(q_up[-1], -1))
        q_down.append(along_z(q_down[-1], 1))
    down, up, _, _ = lax.optimization_barrier((q_down[3], q_up[3], *second))
    q_far = [along_z(down[:, :half], 1), along_z(up[:, half:], -1)]
    lengths = jnp.broadcast_to(new_lengths.astype(BF16)[:, None], (STATS, HEAD))
    new = jnp.concatenate([new_keys, new_values.T, lengths], axis=0)

    def number(*places):
        return jnp.stack([y * NZ + (z + d) % NZ for d in places]).astype(jnp.int32)

    run = functools.partial(attend, hits=hits, stores=[store, store_l, store_r, *far])
    (opposite,) = run(number(4), qs=q_far, n_halves=2)
    got_l, got_r = along_z(opposite[:, :half], 1), along_z(opposite[:, half:], -1)
    for d in (3, 2, 1):
        both = run(number(d, -d), qs=[q_up[d], q_down[d]], n_halves=1)
        to_right, to_left = relay(d == 3, both, got_l, got_r)
        got_l, got_r = along_z(to_right, 1), along_z(to_left, -1)
    own = run(number(0), qs=[queries], n_halves=1, new=(new,))
    head_out = finish(new, own, got_l, got_r)

    rows = jnp.concatenate([head_out, along_y(head_out, 1), along_y(head_out, 2), along_y(head_out, 3)], axis=0)
    pairs = weights.reshape(NX, 2, *out_weight.shape)
    other = lax.dynamic_index_in_dim(pairs, 1 - core, 1, keepdims=False)
    mine = lax.dynamic_index_in_dim(pairs, core, 1, keepdims=False)
    form = "rk,xkc->xrc"
    sent = jnp.einsum(form, rows, other, preferred_element_type=F32).astype(BF16)
    swapped = lax.ppermute(sent, "tp", [(i, i ^ 1) for i in range(2 * NX)])
    summed = lax.optimization_barrier(jnp.einsum(form, rows, mine, preferred_element_type=F32)) + swapped.astype(F32)
    thin = summed.astype(BF16)
    total = at(summed, x)
    for k in range(1, NX):
        total = total + along_x(at(thin, (x + k) % NX), k).astype(F32)
    tile = total.astype(BF16).reshape(NY, TOK, out_weight.shape[1])
    return to_tiles(tile, y, z, t)


def solution(mesh):
    return jax.shard_map(
        shards,
        mesh=mesh,
        in_specs=(
            P("ctx", "tp"),
            P("ctx", "tp"),
            P("ctx", "tp"),
            P("ctx", None, "tp"),
            P("ctx", None, "tp"),
            P("ctx", None, None),
            P("ctx", None),
            P("ctx"),
            P("tp", "ctx"),
        ),
        out_specs=P("tp", "ctx"),
        check_vma=False,
    )
```

```python
import functools

import jax
import jax.numpy as jnp
from jax import lax
from jax.experimental import pallas as pl
from jax.experimental.pallas import tpu as pltpu
from jax.sharding import PartitionSpec as P

HEAD = 128
BLOCK = 128
MOST = 4
TOK = 128
GROUP = 8
ROWS = GROUP * TOK
STORE = 16
NY = 4
NZ = 8
NX = 4
STATS = 16
PART = HEAD + STATS
PAIR = 2 * BLOCK
CHUNK = 8
TAILS = (2, 4, 8)
ROOM = STORE + CHUNK
NEG = -1e30
SCALE2 = 1.4426950408889634 * HEAD**-0.5
VMEM_BYTES = 24 * 1024 * 1024
F32 = jnp.float32
BF16 = jnp.bfloat16


def heads_down(q):
    return jnp.concatenate([q[:, g * HEAD : (g + 1) * HEAD] for g in range(q.shape[1] // HEAD)], axis=0)


def scores(k, q):
    return lax.dot_general(k, q, (((1,), (1,)), ((), ())), preferred_element_type=F32)


def fold8(s):
    return jnp.max(s.reshape(s.shape[0] // 8, 8, s.shape[1]), axis=0)


def stat_rows(m, l):
    high = l.astype(BF16).astype(F32)
    row = lax.broadcasted_iota(jnp.int32, (STATS, m.shape[1]), 0)
    zero = jnp.zeros((STATS, m.shape[1]), F32)
    out = jnp.where(row == 0, m, zero)
    out = jnp.where(row == 1, high, out)
    return jnp.where(row == 2, l - high, out).astype(BF16)


def parts_of(x):
    x = x.astype(F32)
    m = x[HEAD : HEAD + 1]
    l = x[HEAD + 1 : HEAD + 2] + x[HEAD + 2 : HEAD + 3]
    return x[0:HEAD], m, l


def merge(parts):
    top = functools.reduce(jnp.maximum, [m for _, m, _ in parts])
    weights = [jnp.exp2(m - top) for _, m, _ in parts]
    o = sum(w * o for w, (o, _, _) in zip(weights, parts))
    l = sum(w * l for w, (_, _, l) in zip(weights, parts))
    return o, top, l


def take(refs, n):
    return refs[:n], refs[n:]


def attend_kernel(n_seqs, n_halves, with_new, *refs):
    (seq_ref,), refs = take(refs, 1)
    hits, refs = take(refs, NY)
    q_refs, refs = take(refs, n_seqs * n_halves)
    stores, refs = take(refs, NY + 1)
    new, refs = take(refs, int(with_new))
    out, kv, q_raw, q_scr, s_scr, m_scr, acc, places, sems, q_sems = refs

    row = 0
    loads = []
    for i, ref in enumerate(stores):
        size = STORE * PAIR // (1 if i < NY - 1 else 2)
        loads.append(pltpu.make_async_copy(ref.at[pl.ds(0, size), :], kv.at[pl.ds(row, size), :], sems.at[i]))
        row += size
    q_loads = []
    width = ROWS // n_halves
    for i, ref in enumerate(q_refs):
        n, h = i // n_halves, i % n_halves
        q_loads.append(pltpu.make_async_copy(ref, q_raw.at[n, h], q_sems.at[i]))
    for load in q_loads + loads:
        load.start()

    counts = []
    for n in range(n_seqs):
        for i in range(ROOM):
            places[n, i] = 0
        pos = jnp.int32(0)
        seq = seq_ref[n]
        for h, hit in enumerate(hits):
            count = hit[1, seq]
            for j in range(MOST):
                places[n, pos] = h * STORE + hit[0, seq * MOST + j]
                pos = pos + (j < count).astype(jnp.int32)
        places[n, ROOM] = pos

    for load in q_loads:
        load.wait()
    for n in range(n_seqs):
        for g in range(GROUP):
            h, at = divmod(g * HEAD, width)
            q_scr[n, g * TOK : (g + 1) * TOK, :] = q_raw[n, h, :, at : at + HEAD]
    for load in loads:
        load.wait()

    def one(n, carry):
        count = places[n, ROOM]
        full = count // CHUNK
        tail = count - full * CHUNK

        def each(step):
            lax.fori_loop(0, full, lambda i, c: (step(i * CHUNK, CHUNK, False), c)[1], 0)
            low = 0
            for size in TAILS:

                @pl.when((tail > low) & (tail <= size))
                def _(size=size):
                    step(full * CHUNK, size, True)

                low = size

        def rows_of(base, size, shift):
            first = [pl.multiple_of(places[n, base + i] * PAIR + shift, BLOCK) for i in range(size)]
            return [kv[pl.ds(at, BLOCK), :] for at in first]

        q = q_scr[n]
        m_scr[...] = jnp.full_like(m_scr, NEG)
        acc[...] = jnp.zeros_like(acc)

        def first(base, size, masked):
            s = scores(jnp.concatenate(rows_of(base, size, 0), axis=0), q)
            if masked:
                key = lax.broadcasted_iota(jnp.int32, s.shape, 0)
                s = jnp.where(key < tail * BLOCK, s, NEG)
            s_scr[pl.ds(base, size)] = s.reshape(size, BLOCK, ROWS)
            m_scr[...] = jnp.maximum(m_scr[...], fold8(s))

        each(first)
        if with_new:
            s = scores(new[0][0:BLOCK, :], q)
            key = lax.broadcasted_iota(jnp.int32, s.shape, 0)
            tok = lax.broadcasted_iota(jnp.int32, s.shape, 1) % TOK
            s = jnp.where(key <= tok, s, NEG)
            s_scr[STORE] = s
            m_scr[...] = jnp.maximum(m_scr[...], fold8(s))

        m = (jnp.max(m_scr[...], axis=0, keepdims=True) * SCALE2).astype(BF16).astype(F32)

        def weigh(s, v):
            p = jnp.exp2(s * SCALE2 - m).astype(BF16)
            v = jnp.concatenate([v, jnp.ones((STATS, v.shape[1]), BF16)], axis=0)
            acc[...] += jnp.dot(v, p, preferred_element_type=F32)

        def second(base, size, masked):
            s = s_scr[pl.ds(base, size)].reshape(size * BLOCK, ROWS)
            weigh(s, jnp.concatenate(rows_of(base, size, BLOCK), axis=1))

        each(second)
        if with_new:
            weigh(s_scr[STORE], new[0][BLOCK:PAIR, :])
        out[n, 0:HEAD, :] = acc[0:HEAD, :].astype(BF16)
        out[n, HEAD:PART, :] = stat_rows(m, acc[HEAD : HEAD + 1, :])
        return carry

    lax.fori_loop(0, n_seqs, one, 0)


def attend(seqs, hits, qs, n_halves, stores, new=()):
    n_seqs = len(qs) // n_halves
    smem = pl.BlockSpec(memory_space=pltpu.SMEM)
    vmem = pl.BlockSpec(memory_space=pltpu.VMEM)
    anywhere = pl.BlockSpec(memory_space=pl.ANY)
    work = n_seqs * 8
    return pl.pallas_call(
        functools.partial(attend_kernel, n_seqs, n_halves, len(new) > 0),
        out_shape=jax.ShapeDtypeStruct((n_seqs, PART, ROWS), BF16),
        in_specs=[smem] * (1 + NY) + [anywhere] * (len(qs) + len(stores)) + [vmem] * len(new),
        out_specs=vmem,
        scratch_shapes=[
            pltpu.VMEM((NY * STORE * PAIR, HEAD), BF16),
            pltpu.VMEM((n_seqs, n_halves, TOK, ROWS // n_halves), BF16),
            pltpu.VMEM((n_seqs, ROWS, HEAD), BF16),
            pltpu.VMEM((STORE + 1, BLOCK, ROWS), F32),
            pltpu.VMEM((8, ROWS), F32),
            pltpu.VMEM((PART, ROWS), F32),
            pltpu.SMEM((n_seqs, ROOM + 1), jnp.int32),
            pltpu.SemaphoreType.DMA((NY + 1,)),
            pltpu.SemaphoreType.DMA((len(qs),)),
        ],
        compiler_params=pltpu.CompilerParams(vmem_limit_bytes=VMEM_BYTES),
        cost_estimate=pl.CostEstimate(
            flops=work * 4 * BLOCK * ROWS * HEAD,
            bytes_accessed=5 * 2**20,
            transcendentals=work * BLOCK * ROWS,
        ),
    )(seqs, *hits, *qs, *stores, *new)


def relay_kernel(halves, own, got_a, got_b, out_a, out_b):
    half = ROWS // 2
    for n, (got, out) in enumerate(((got_a, out_a), (got_b, out_b))):
        cols = slice(0, ROWS)
        if halves:
            cols = slice(n * half, (n + 1) * half)
            rest = slice((1 - n) * half, (2 - n) * half)
            out[:, rest] = own[n, :, rest]
        o, m, l = merge([parts_of(own[n, :, cols]), parts_of(got[...])])
        out[0:HEAD, cols] = o.astype(BF16)
        out[HEAD:PART, cols] = stat_rows(m, l)


def relay(halves, own, got_a, got_b):
    vmem = pl.BlockSpec(memory_space=pltpu.VMEM)
    return pl.pallas_call(
        functools.partial(relay_kernel, halves),
        out_shape=[jax.ShapeDtypeStruct((PART, ROWS), BF16)] * 2,
        in_specs=[vmem] * 3,
        out_specs=[vmem] * 2,
        compiler_params=pltpu.CompilerParams(vmem_limit_bytes=VMEM_BYTES),
        cost_estimate=pl.CostEstimate(flops=8 * PART * ROWS, bytes_accessed=2 * 2**20, transcendentals=4 * ROWS),
    )(own, got_a, got_b)


def finish_kernel(new, own, left, right, out):
    o, _, l = merge([parts_of(own[0]), parts_of(left[...]), parts_of(right[...])])
    attended = o / l
    tok = lax.broadcasted_iota(jnp.int32, attended.shape, 1) % TOK
    length = new[PAIR : PAIR + STATS, :].astype(F32)[0:1, 0:1]
    attended = jnp.where(tok.astype(F32) < length, attended, 0.0)
    for g in range(GROUP):
        out[:, g * HEAD : (g + 1) * HEAD] = attended[:, g * TOK : (g + 1) * TOK].T.astype(BF16)


def finish(new, own, left, right):
    vmem = pl.BlockSpec(memory_space=pltpu.VMEM)
    return pl.pallas_call(
        finish_kernel,
        out_shape=jax.ShapeDtypeStruct((TOK, ROWS), BF16),
        in_specs=[vmem] * 4,
        out_specs=vmem,
        compiler_params=pltpu.CompilerParams(vmem_limit_bytes=VMEM_BYTES),
        cost_estimate=pl.CostEstimate(flops=8 * PART * ROWS, bytes_accessed=2**20, transcendentals=4 * ROWS),
    )(new, own, left, right)


def along_z(x, k):
    return lax.ppermute(x, "ctx", [(y * NZ + z, y * NZ + (z + k) % NZ) for y in range(NY) for z in range(NZ)])


def along_y(x, k):
    return lax.ppermute(x, "ctx", [(y * NZ + z, (y + k) % NY * NZ + z) for y in range(NY) for z in range(NZ)])


def along_x(x, k):
    return lax.ppermute(x, "tp", [(2 * i + c, 2 * ((i + k) % NX) + c) for i in range(NX) for c in range(2)])


def at(x, i):
    return lax.dynamic_index_in_dim(x, i, 0, keepdims=False)


def to_tiles(tile):
    pairs = []
    for y in range(NY):
        for z in range(NZ):
            for x in range(NX):
                for c in range(2):
                    source = (y * NZ + z) * 2 * NX + 2 * x + c
                    pairs.append((source, (x * NZ + z) * 2 * NX + 2 * y + c))
    return lax.ppermute(tile, ("ctx", "tp"), pairs)


def shards(
    queries,
    new_keys,
    new_values,
    store_keys,
    store_values,
    hit_blocks,
    hit_counts,
    new_lengths,
    out_weight,
):
    me = lax.axis_index("ctx")
    t = lax.axis_index("tp")
    y, z = me // NZ, me % NZ
    x, core = t // 2, t % 2

    blocks = jnp.concatenate([store_keys, jnp.swapaxes(store_values, 1, 2)], axis=1).reshape(STORE * PAIR, HEAD)
    lists = jnp.stack([hit_blocks.reshape(-1), jnp.pad(hit_counts[0], (0, 128 - hit_counts.shape[1]))])
    store = jnp.concatenate([blocks, jnp.pad(lists, ((0, STATS - 2), (0, 0))).astype(BF16)], axis=0)
    store_l, store_r = along_y(store, 1), along_y(store, -1)
    middle = STORE // 2 * PAIR
    second = [store_l[:middle], store_r[middle:]]
    far = [along_y(second[0], 1), along_y(second[1], -1)]

    def listed(x):
        return x[-STATS : 2 - STATS].astype(jnp.int32)

    hits = [lists, listed(store_l), listed(store_r), listed(far[1])]

    half = ROWS // 2
    q_up = [queries]
    q_down = [queries]
    for _ in range(3):
        q_up.append(along_z(q_up[-1], -1))
        q_down.append(along_z(q_down[-1], 1))
    down, up, _, _, out_weight = lax.optimization_barrier((q_down[3], q_up[3], *second, out_weight))
    q_far = [along_z(down[:, :half], 1), along_z(up[:, half:], -1)]
    weights = lax.all_gather(
        out_weight,
        "ctx",
        axis=0,
        tiled=False,
        axis_index_groups=[[yy * NZ + zz for yy in range(NY)] for zz in range(NZ)],
    )

    lengths = jnp.broadcast_to(new_lengths.astype(BF16)[:, None], (STATS, HEAD))
    new = jnp.concatenate([new_keys, new_values.T, lengths], axis=0)

    def number(*places):
        return jnp.stack([y * NZ + (z + d) % NZ for d in places]).astype(jnp.int32)

    run = functools.partial(attend, hits=hits, stores=[store, store_l, store_r, *far])
    (opposite,) = run(number(4), qs=q_far, n_halves=2)
    got_l, got_r = along_z(opposite[:, :half], 1), along_z(opposite[:, half:], -1)
    for d in (3, 2, 1):
        both = run(number(d, -d), qs=[q_up[d], q_down[d]], n_halves=1)
        to_right, to_left = relay(d == 3, both, got_l, got_r)
        got_l, got_r = along_z(to_right, 1), along_z(to_left, -1)
    own = run(number(0), qs=[queries], n_halves=1, new=(new,))
    head_out = finish(new, own, got_l, got_r)

    rows = jnp.zeros((NZ, TOK, ROWS), BF16)

    def put(rows, piece, place, column=0):
        return lax.dynamic_update_slice(rows, piece[None], ((z + place) % NZ, 0, column))

    rows = put(rows, head_out, 0)
    up = down = head_out
    for d in (1, 2, 3):
        up, down = along_z(up, -1), along_z(down, 1)
        rows = put(put(rows, up, d), down, -d)
    far_l, far_r = along_z(down[:, :half], 1), along_z(up[:, half:], -1)
    rows = put(put(rows, far_l, 4), far_r, 4, half)

    def project(i):
        mine = lax.dynamic_slice_in_dim(rows, i * NZ // 2, NZ // 2, 0).reshape(NZ // 2 * TOK, ROWS)
        return jnp.einsum("rk,xkc->xrc", mine, weights, preferred_element_type=F32)

    sent = project(1 - core).astype(BF16)
    swapped = lax.ppermute(sent, "tp", [(i, i ^ 1) for i in range(2 * NX)])
    summed = lax.optimization_barrier(project(core)) + swapped.astype(F32)
    thin = summed.astype(BF16)
    total = at(summed, x)
    for k in range(1, NX):
        total = total + along_x(at(thin, (x + k) % NX), k).astype(F32)
    return to_tiles(total.astype(BF16))


def solution(mesh):
    return jax.shard_map(
        shards,
        mesh=mesh,
        in_specs=(
            P("ctx", "tp"),
            P("ctx", "tp"),
            P("ctx", "tp"),
            P("ctx", None, "tp"),
            P("ctx", None, "tp"),
            P("ctx", None, None),
            P("ctx", None),
            P("ctx"),
            P("tp", "ctx"),
        ),
        out_specs=P("tp", "ctx"),
        check_vma=False,
    )
```

```python
import functools

import jax
import jax.numpy as jnp
from jax import lax
from jax.experimental import pallas as pl
from jax.experimental.pallas import tpu as pltpu
from jax.sharding import PartitionSpec as P

HEAD = 128
BLOCK = 128
MOST = 4
TOK = 128
GROUP = 8
ROWS = GROUP * TOK
STORE = 16
NY = 4
NZ = 8
NX = 4
STATS = 16
PART = HEAD + STATS
PAIR = 2 * BLOCK
CHUNK = 8
TAILS = (2, 4, 8)
ROOM = STORE + CHUNK
NEG = -1e30
SCALE2 = 1.4426950408889634 * HEAD**-0.5
VMEM_BYTES = 24 * 1024 * 1024
F32 = jnp.float32
BF16 = jnp.bfloat16


def heads_down(q):
    return jnp.concatenate([q[:, g * HEAD : (g + 1) * HEAD] for g in range(q.shape[1] // HEAD)], axis=0)


def scores(k, q):
    return lax.dot_general(k, q, (((1,), (1,)), ((), ())), preferred_element_type=F32)


def fold8(s):
    return jnp.max(s.reshape(s.shape[0] // 8, 8, s.shape[1]), axis=0)


def stat_rows(m, l):
    high = l.astype(BF16).astype(F32)
    row = lax.broadcasted_iota(jnp.int32, (STATS, m.shape[1]), 0)
    zero = jnp.zeros((STATS, m.shape[1]), F32)
    out = jnp.where(row == 0, m, zero)
    out = jnp.where(row == 1, high, out)
    return jnp.where(row == 2, l - high, out).astype(BF16)


def parts_of(x):
    x = x.astype(F32)
    m = x[HEAD : HEAD + 1]
    l = x[HEAD + 1 : HEAD + 2] + x[HEAD + 2 : HEAD + 3]
    return x[0:HEAD], m, l


def merge(parts):
    top = functools.reduce(jnp.maximum, [m for _, m, _ in parts])
    weights = [jnp.exp2(m - top) for _, m, _ in parts]
    o = sum(w * o for w, (o, _, _) in zip(weights, parts))
    l = sum(w * l for w, (_, _, l) in zip(weights, parts))
    return o, top, l


def take(refs, n):
    return refs[:n], refs[n:]


def attend_kernel(n_seqs, n_halves, with_new, *refs):
    (seq_ref,), refs = take(refs, 1)
    hits, refs = take(refs, NY)
    q_refs, refs = take(refs, n_seqs * n_halves)
    stores, refs = take(refs, NY + 1)
    new, refs = take(refs, int(with_new))
    out, kv, q_raw, q_scr, s_scr, m_scr, acc, places, sems, q_sems = refs

    row = 0
    loads = []
    for i, ref in enumerate(stores):
        size = STORE * PAIR // (1 if i < NY - 1 else 2)
        loads.append(pltpu.make_async_copy(ref.at[pl.ds(0, size), :], kv.at[pl.ds(row, size), :], sems.at[i]))
        row += size
    q_loads = []
    width = ROWS // n_halves
    for i, ref in enumerate(q_refs):
        n, h = i // n_halves, i % n_halves
        q_loads.append(pltpu.make_async_copy(ref, q_raw.at[n, h], q_sems.at[i]))
    for load in q_loads + loads:
        load.start()

    counts = []
    for n in range(n_seqs):
        for i in range(ROOM):
            places[n, i] = 0
        pos = jnp.int32(0)
        seq = seq_ref[n]
        for h, hit in enumerate(hits):
            count = hit[1, seq]
            for j in range(MOST):
                places[n, pos] = h * STORE + hit[0, seq * MOST + j]
                pos = pos + (j < count).astype(jnp.int32)
        places[n, ROOM] = pos

    for load in q_loads:
        load.wait()
    for n in range(n_seqs):
        for g in range(GROUP):
            h, at = divmod(g * HEAD, width)
            q_scr[n, g * TOK : (g + 1) * TOK, :] = q_raw[n, h, :, at : at + HEAD]
    for load in loads:
        load.wait()

    def one(n, carry):
        count = places[n, ROOM]
        full = count // CHUNK
        tail = count - full * CHUNK

        def each(step):
            lax.fori_loop(0, full, lambda i, c: (step(i * CHUNK, CHUNK, False), c)[1], 0)
            low = 0
            for size in TAILS:

                @pl.when((tail > low) & (tail <= size))
                def _(size=size):
                    step(full * CHUNK, size, True)

                low = size

        def rows_of(base, size, shift):
            first = [pl.multiple_of(places[n, base + i] * PAIR + shift, BLOCK) for i in range(size)]
            return [kv[pl.ds(at, BLOCK), :] for at in first]

        q = q_scr[n]
        m_scr[...] = jnp.full_like(m_scr, NEG)
        acc[...] = jnp.zeros_like(acc)

        def first(base, size, masked):
            s = scores(jnp.concatenate(rows_of(base, size, 0), axis=0), q)
            if masked:
                key = lax.broadcasted_iota(jnp.int32, s.shape, 0)
                s = jnp.where(key < tail * BLOCK, s, NEG)
            s_scr[pl.ds(base, size)] = s.reshape(size, BLOCK, ROWS)
            m_scr[...] = jnp.maximum(m_scr[...], fold8(s))

        each(first)
        if with_new:
            s = scores(new[0][0:BLOCK, :], q)
            key = lax.broadcasted_iota(jnp.int32, s.shape, 0)
            tok = lax.broadcasted_iota(jnp.int32, s.shape, 1) % TOK
            s = jnp.where(key <= tok, s, NEG)
            s_scr[STORE] = s
            m_scr[...] = jnp.maximum(m_scr[...], fold8(s))

        m = (jnp.max(m_scr[...], axis=0, keepdims=True) * SCALE2).astype(BF16).astype(F32)

        def weigh(s, v):
            p = jnp.exp2(s * SCALE2 - m).astype(BF16)
            v = jnp.concatenate([v, jnp.ones((STATS, v.shape[1]), BF16)], axis=0)
            acc[...] += jnp.dot(v, p, preferred_element_type=F32)

        def second(base, size, masked):
            s = s_scr[pl.ds(base, size)].reshape(size * BLOCK, ROWS)
            weigh(s, jnp.concatenate(rows_of(base, size, BLOCK), axis=1))

        each(second)
        if with_new:
            weigh(s_scr[STORE], new[0][BLOCK:PAIR, :])
        out[n, 0:HEAD, :] = acc[0:HEAD, :].astype(BF16)
        out[n, HEAD:PART, :] = stat_rows(m, acc[HEAD : HEAD + 1, :])
        return carry

    lax.fori_loop(0, n_seqs, one, 0)


def attend(seqs, hits, qs, n_halves, stores, new=()):
    n_seqs = len(qs) // n_halves
    smem = pl.BlockSpec(memory_space=pltpu.SMEM)
    vmem = pl.BlockSpec(memory_space=pltpu.VMEM)
    anywhere = pl.BlockSpec(memory_space=pl.ANY)
    work = n_seqs * 8
    return pl.pallas_call(
        functools.partial(attend_kernel, n_seqs, n_halves, len(new) > 0),
        out_shape=jax.ShapeDtypeStruct((n_seqs, PART, ROWS), BF16),
        in_specs=[smem] * (1 + NY) + [anywhere] * (len(qs) + len(stores)) + [vmem] * len(new),
        out_specs=vmem,
        scratch_shapes=[
            pltpu.VMEM((NY * STORE * PAIR, HEAD), BF16),
            pltpu.VMEM((n_seqs, n_halves, TOK, ROWS // n_halves), BF16),
            pltpu.VMEM((n_seqs, ROWS, HEAD), BF16),
            pltpu.VMEM((STORE + 1, BLOCK, ROWS), F32),
            pltpu.VMEM((8, ROWS), F32),
            pltpu.VMEM((PART, ROWS), F32),
            pltpu.SMEM((n_seqs, ROOM + 1), jnp.int32),
            pltpu.SemaphoreType.DMA((NY + 1,)),
            pltpu.SemaphoreType.DMA((len(qs),)),
        ],
        compiler_params=pltpu.CompilerParams(vmem_limit_bytes=VMEM_BYTES),
        cost_estimate=pl.CostEstimate(
            flops=work * 4 * BLOCK * ROWS * HEAD,
            bytes_accessed=5 * 2**20,
            transcendentals=work * BLOCK * ROWS,
        ),
    )(seqs, *hits, *qs, *stores, *new)


def relay_kernel(halves, own, got_a, got_b, out_a, out_b):
    half = ROWS // 2
    for n, (got, out) in enumerate(((got_a, out_a), (got_b, out_b))):
        cols = slice(0, ROWS)
        if halves:
            cols = slice(n * half, (n + 1) * half)
            rest = slice((1 - n) * half, (2 - n) * half)
            out[:, rest] = own[n, :, rest]
        o, m, l = merge([parts_of(own[n, :, cols]), parts_of(got[...])])
        out[0:HEAD, cols] = o.astype(BF16)
        out[HEAD:PART, cols] = stat_rows(m, l)


def relay(halves, own, got_a, got_b):
    vmem = pl.BlockSpec(memory_space=pltpu.VMEM)
    return pl.pallas_call(
        functools.partial(relay_kernel, halves),
        out_shape=[jax.ShapeDtypeStruct((PART, ROWS), BF16)] * 2,
        in_specs=[vmem] * 3,
        out_specs=[vmem] * 2,
        compiler_params=pltpu.CompilerParams(vmem_limit_bytes=VMEM_BYTES),
        cost_estimate=pl.CostEstimate(flops=8 * PART * ROWS, bytes_accessed=2 * 2**20, transcendentals=4 * ROWS),
    )(own, got_a, got_b)


def finish_kernel(new, own, left, right, out):
    o, _, l = merge([parts_of(own[0]), parts_of(left[...]), parts_of(right[...])])
    attended = o / l
    tok = lax.broadcasted_iota(jnp.int32, attended.shape, 1) % TOK
    length = new[PAIR : PAIR + STATS, :].astype(F32)[0:1, 0:1]
    attended = jnp.where(tok.astype(F32) < length, attended, 0.0)
    for g in range(GROUP):
        out[:, g * HEAD : (g + 1) * HEAD] = attended[:, g * TOK : (g + 1) * TOK].T.astype(BF16)


def finish(new, own, left, right):
    vmem = pl.BlockSpec(memory_space=pltpu.VMEM)
    return pl.pallas_call(
        finish_kernel,
        out_shape=jax.ShapeDtypeStruct((TOK, ROWS), BF16),
        in_specs=[vmem] * 4,
        out_specs=vmem,
        compiler_params=pltpu.CompilerParams(vmem_limit_bytes=VMEM_BYTES),
        cost_estimate=pl.CostEstimate(flops=8 * PART * ROWS, bytes_accessed=2**20, transcendentals=4 * ROWS),
    )(new, own, left, right)


def along_z(x, k):
    return lax.ppermute(x, "ctx", [(y * NZ + z, y * NZ + (z + k) % NZ) for y in range(NY) for z in range(NZ)])


def along_y(x, k):
    return lax.ppermute(x, "ctx", [(y * NZ + z, (y + k) % NY * NZ + z) for y in range(NY) for z in range(NZ)])


def along_x(x, k):
    return lax.ppermute(x, "tp", [(2 * i + c, 2 * ((i + k) % NX) + c) for i in range(NX) for c in range(2)])


def at(x, i):
    return lax.dynamic_index_in_dim(x, i, 0, keepdims=False)


def to_tile(piece, r):
    pairs = []
    for y in range(NY):
        for z in range(NZ):
            for x in range(NX):
                for c in range(2):
                    source = (y * NZ + z) * 2 * NX + 2 * x + c
                    pairs.append((source, ((x + r) % NY * NZ + z) * 2 * NX + 2 * y + c))
    return lax.ppermute(piece, ("ctx", "tp"), pairs)


def shards(
    queries,
    new_keys,
    new_values,
    store_keys,
    store_values,
    hit_blocks,
    hit_counts,
    new_lengths,
    out_weight,
):
    me = lax.axis_index("ctx")
    t = lax.axis_index("tp")
    y, z = me // NZ, me % NZ
    x, core = t // 2, t % 2

    blocks = jnp.concatenate([store_keys, jnp.swapaxes(store_values, 1, 2)], axis=1).reshape(STORE * PAIR, HEAD)
    lists = jnp.stack([hit_blocks.reshape(-1), jnp.pad(hit_counts[0], (0, 128 - hit_counts.shape[1]))])
    store = jnp.concatenate([blocks, jnp.pad(lists, ((0, STATS - 2), (0, 0))).astype(BF16)], axis=0)
    store_l, store_r = along_y(store, 1), along_y(store, -1)
    middle = STORE // 2 * PAIR
    second = [store_l[:middle], store_r[middle:]]
    far = [along_y(second[0], 1), along_y(second[1], -1)]

    def listed(x):
        return x[-STATS : 2 - STATS].astype(jnp.int32)

    hits = [lists, listed(store_l), listed(store_r), listed(far[1])]

    half = ROWS // 2
    q_up = [queries]
    q_down = [queries]
    for _ in range(3):
        q_up.append(along_z(q_up[-1], -1))
        q_down.append(along_z(q_down[-1], 1))
    down, up, _, _, out_weight = lax.optimization_barrier((q_down[3], q_up[3], *second, out_weight))
    q_far = [along_z(down[:, :half], 1), along_z(up[:, half:], -1)]
    weights = lax.all_gather(
        out_weight,
        "ctx",
        axis=0,
        tiled=False,
        axis_index_groups=[[yy * NZ + zz for yy in range(NY)] for zz in range(NZ)],
    )

    lengths = jnp.broadcast_to(new_lengths.astype(BF16)[:, None], (STATS, HEAD))
    new = jnp.concatenate([new_keys, new_values.T, lengths], axis=0)

    def number(*places):
        return jnp.stack([y * NZ + (z + d) % NZ for d in places]).astype(jnp.int32)

    run = functools.partial(attend, hits=hits, stores=[store, store_l, store_r, *far])
    (opposite,) = run(number(4), qs=q_far, n_halves=2)
    got_l, got_r = along_z(opposite[:, :half], 1), along_z(opposite[:, half:], -1)
    for d in (3, 2, 1):
        both = run(number(d, -d), qs=[q_up[d], q_down[d]], n_halves=1)
        to_right, to_left = relay(d == 3, both, got_l, got_r)
        got_l, got_r = along_z(to_right, 1), along_z(to_left, -1)
    own = run(number(0), qs=[queries], n_halves=1, new=(new,))
    head_out = finish(new, own, got_l, got_r)

    columns = out_weight.shape[1]
    partial = jnp.zeros((NY, NZ, TOK, columns), BF16)

    def project(partial, pieces, places):
        rows = jnp.concatenate(pieces, axis=0)
        part = jnp.einsum("rk,xkc->xrc", rows, weights, preferred_element_type=F32).astype(BF16)
        part = part.reshape(NY, len(pieces), TOK, columns)
        for i, place in enumerate(places):
            partial = lax.dynamic_update_slice(partial, part[:, i : i + 1], (0, (z + place) % NZ, 0, 0))
        return partial

    up = down = head_out
    pieces, places = [head_out], [0]
    for d in (1, 2, 3, 4):
        if d > 1:
            up, down, partial = lax.optimization_barrier((up, down, partial))
        if d < 4:
            next_up, next_down = along_z(up, -1), along_z(down, 1)
            arriving = [next_up, next_down], [d, -d]
        else:
            far_l, far_r = along_z(down[:, :half], 1), along_z(up[:, half:], -1)
            arriving = [jnp.concatenate([far_l, far_r], axis=1)], [4]
        partial = project(partial, pieces, places)
        up, down = next_up, next_down
        pieces, places = arriving
    partial = project(partial, pieces, places)

    def share(i):
        return lax.dynamic_slice_in_dim(partial, i * (NZ // 2), NZ // 2, 1)

    swapped = lax.ppermute(share(1 - core), "tp", [(i, i ^ 1) for i in range(2 * NX)])
    summed = (share(core).astype(F32) + swapped.astype(F32)).astype(BF16)
    summed = summed.reshape(NY, NZ // 2 * TOK, columns)
    total = 0.0
    for r in range(NY):
        total = total + to_tile(at(summed, (x + r) % NY), r).astype(F32)
    return total.astype(BF16)


def solution(mesh):
    return jax.shard_map(
        shards,
        mesh=mesh,
        in_specs=(
            P("ctx", "tp"),
            P("ctx", "tp"),
            P("ctx", "tp"),
            P("ctx", None, "tp"),
            P("ctx", None, "tp"),
            P("ctx", None, None),
            P("ctx", None),
            P("ctx"),
            P("tp", "ctx"),
        ),
        out_specs=P("tp", "ctx"),
        check_vma=False,
    )
```

```python
import functools

import jax
import jax.numpy as jnp
from jax import lax
from jax.experimental import pallas as pl
from jax.experimental.pallas import tpu as pltpu
from jax.sharding import PartitionSpec as P

HEAD = 128
BLOCK = 128
MOST = 4
TOK = 128
GROUP = 8
ROWS = GROUP * TOK
STORE = 16
NY = 4
NZ = 8
NX = 4
STATS = 16
PART = HEAD + STATS
PAIR = 2 * BLOCK
CHUNK = 8
TAILS = (2, 4, 8)
ROOM = STORE + CHUNK
NEG = -1e30
SCALE2 = 1.4426950408889634 * HEAD**-0.5
VMEM_BYTES = 60 * 1024 * 1024
MERGE_BYTES = 16 * 1024 * 1024
F32 = jnp.float32
BF16 = jnp.bfloat16


def heads_down(q):
    return jnp.concatenate([q[:, g * HEAD : (g + 1) * HEAD] for g in range(q.shape[1] // HEAD)], axis=0)


def scores(k, q):
    return lax.dot_general(k, q, (((1,), (1,)), ((), ())), preferred_element_type=F32)


def fold8(s):
    return jnp.max(s.reshape(s.shape[0] // 8, 8, s.shape[1]), axis=0)


def stat_rows(m, l):
    high = l.astype(BF16).astype(F32)
    row = lax.broadcasted_iota(jnp.int32, (STATS, m.shape[1]), 0)
    zero = jnp.zeros((STATS, m.shape[1]), F32)
    out = jnp.where(row == 0, m, zero)
    out = jnp.where(row == 1, high, out)
    return jnp.where(row == 2, l - high, out).astype(BF16)


def parts_of(x):
    x = x.astype(F32)
    m = x[HEAD : HEAD + 1]
    l = x[HEAD + 1 : HEAD + 2] + x[HEAD + 2 : HEAD + 3]
    return x[0:HEAD], m, l


def merge(parts):
    top = functools.reduce(jnp.maximum, [m for _, m, _ in parts])
    weights = [jnp.exp2(m - top) for _, m, _ in parts]
    o = sum(w * o for w, (o, _, _) in zip(weights, parts))
    l = sum(w * l for w, (_, _, l) in zip(weights, parts))
    return o, top, l


def take(refs, n):
    return refs[:n], refs[n:]


def attend_kernel(n_seqs, n_halves, with_new, *refs):
    (seq_ref,), refs = take(refs, 1)
    hits, refs = take(refs, NY)
    q_refs, refs = take(refs, n_seqs * n_halves)
    stores, refs = take(refs, NY + 1)
    new, refs = take(refs, int(with_new))
    out, kv, q_raw, q_scr, s_scr, m_scr, acc, places, sems, q_sems = refs

    row = 0
    loads = []
    for i, ref in enumerate(stores):
        size = STORE * PAIR // (1 if i < NY - 1 else 2)
        loads.append(pltpu.make_async_copy(ref.at[pl.ds(0, size), :], kv.at[pl.ds(row, size), :], sems.at[i]))
        row += size
    q_loads = []
    width = ROWS // n_halves
    for i, ref in enumerate(q_refs):
        n, h = i // n_halves, i % n_halves
        q_loads.append(pltpu.make_async_copy(ref, q_raw.at[n, h], q_sems.at[i]))
    for load in q_loads + loads:
        load.start()

    counts = []
    for n in range(n_seqs):
        for i in range(ROOM):
            places[n, i] = 0
        pos = jnp.int32(0)
        seq = seq_ref[n]
        for h, hit in enumerate(hits):
            count = hit[1, seq]
            for j in range(MOST):
                places[n, pos] = h * STORE + hit[0, seq * MOST + j]
                pos = pos + (j < count).astype(jnp.int32)
        places[n, ROOM] = pos

    for load in q_loads:
        load.wait()
    for n in range(n_seqs):
        for g in range(GROUP):
            h, at = divmod(g * HEAD, width)
            q_scr[n, g * TOK : (g + 1) * TOK, :] = q_raw[n, h, :, at : at + HEAD]
    for load in loads:
        load.wait()

    def one(n, carry):
        count = places[n, ROOM]
        full = count // CHUNK
        tail = count - full * CHUNK

        def each(step):
            lax.fori_loop(0, full, lambda i, c: (step(i * CHUNK, CHUNK, False), c)[1], 0)
            low = 0
            for size in TAILS:

                @pl.when((tail > low) & (tail <= size))
                def _(size=size):
                    step(full * CHUNK, size, True)

                low = size

        def rows_of(base, size, shift):
            first = [pl.multiple_of(places[n, base + i] * PAIR + shift, BLOCK) for i in range(size)]
            return [kv[pl.ds(at, BLOCK), :] for at in first]

        q = q_scr[n]
        m_scr[...] = jnp.full_like(m_scr, NEG)
        acc[...] = jnp.zeros_like(acc)

        def first(base, size, masked):
            s = scores(jnp.concatenate(rows_of(base, size, 0), axis=0), q)
            if masked:
                key = lax.broadcasted_iota(jnp.int32, s.shape, 0)
                s = jnp.where(key < tail * BLOCK, s, NEG)
            s_scr[pl.ds(base, size)] = s.reshape(size, BLOCK, ROWS)
            m_scr[...] = jnp.maximum(m_scr[...], fold8(s))

        each(first)
        if with_new:
            s = scores(new[0][0:BLOCK, :], q)
            key = lax.broadcasted_iota(jnp.int32, s.shape, 0)
            tok = lax.broadcasted_iota(jnp.int32, s.shape, 1) % TOK
            s = jnp.where(key <= tok, s, NEG)
            s_scr[STORE] = s
            m_scr[...] = jnp.maximum(m_scr[...], fold8(s))

        m = (jnp.max(m_scr[...], axis=0, keepdims=True) * SCALE2).astype(BF16).astype(F32)

        def weigh(s, v):
            p = jnp.exp2(s * SCALE2 - m).astype(BF16)
            v = jnp.concatenate([v, jnp.ones((STATS, v.shape[1]), BF16)], axis=0)
            acc[...] += jnp.dot(v, p, preferred_element_type=F32)

        def second(base, size, masked):
            s = s_scr[pl.ds(base, size)].reshape(size * BLOCK, ROWS)
            weigh(s, jnp.concatenate(rows_of(base, size, BLOCK), axis=1))

        each(second)
        if with_new:
            weigh(s_scr[STORE], new[0][BLOCK:PAIR, :])
        out[n, 0:HEAD, :] = acc[0:HEAD, :].astype(BF16)
        out[n, HEAD:PART, :] = stat_rows(m, acc[HEAD : HEAD + 1, :])
        return carry

    lax.fori_loop(0, n_seqs, one, 0)


def attend(seqs, hits, qs, n_halves, stores, new=()):
    n_seqs = len(qs) // n_halves
    smem = pl.BlockSpec(memory_space=pltpu.SMEM)
    vmem = pl.BlockSpec(memory_space=pltpu.VMEM)
    anywhere = pl.BlockSpec(memory_space=pl.ANY)
    work = n_seqs * 8
    return pl.pallas_call(
        functools.partial(attend_kernel, n_seqs, n_halves, len(new) > 0),
        out_shape=jax.ShapeDtypeStruct((n_seqs, PART, ROWS), BF16),
        in_specs=[smem] * (1 + NY) + [anywhere] * (len(qs) + len(stores)) + [vmem] * len(new),
        out_specs=vmem,
        scratch_shapes=[
            pltpu.VMEM((NY * STORE * PAIR, HEAD), BF16),
            pltpu.VMEM((n_seqs, n_halves, TOK, ROWS // n_halves), BF16),
            pltpu.VMEM((n_seqs, ROWS, HEAD), BF16),
            pltpu.VMEM((STORE + 1, BLOCK, ROWS), F32),
            pltpu.VMEM((8, ROWS), F32),
            pltpu.VMEM((PART, ROWS), F32),
            pltpu.SMEM((n_seqs, ROOM + 1), jnp.int32),
            pltpu.SemaphoreType.DMA((NY + 1,)),
            pltpu.SemaphoreType.DMA((len(qs),)),
        ],
        compiler_params=pltpu.CompilerParams(vmem_limit_bytes=VMEM_BYTES),
        cost_estimate=pl.CostEstimate(
            flops=work * 4 * BLOCK * ROWS * HEAD,
            bytes_accessed=5 * 2**20,
            transcendentals=work * BLOCK * ROWS,
        ),
    )(seqs, *hits, *qs, *stores, *new)


def relay_kernel(halves, own, got_a, got_b, out_a, out_b):
    half = ROWS // 2
    for n, (got, out) in enumerate(((got_a, out_a), (got_b, out_b))):
        cols = slice(0, ROWS)
        if halves:
            cols = slice(n * half, (n + 1) * half)
            rest = slice((1 - n) * half, (2 - n) * half)
            out[:, rest] = own[n, :, rest]
        o, m, l = merge([parts_of(own[n, :, cols]), parts_of(got[...])])
        out[0:HEAD, cols] = o.astype(BF16)
        out[HEAD:PART, cols] = stat_rows(m, l)


def relay(halves, own, got_a, got_b):
    vmem = pl.BlockSpec(memory_space=pltpu.VMEM)
    return pl.pallas_call(
        functools.partial(relay_kernel, halves),
        out_shape=[jax.ShapeDtypeStruct((PART, ROWS), BF16)] * 2,
        in_specs=[vmem] * 3,
        out_specs=[vmem] * 2,
        compiler_params=pltpu.CompilerParams(vmem_limit_bytes=MERGE_BYTES),
        cost_estimate=pl.CostEstimate(flops=8 * PART * ROWS, bytes_accessed=2 * 2**20, transcendentals=4 * ROWS),
    )(own, got_a, got_b)


def finish_kernel(new, own, left, right, out):
    o, _, l = merge([parts_of(own[0]), parts_of(left[...]), parts_of(right[...])])
    attended = o / l
    tok = lax.broadcasted_iota(jnp.int32, attended.shape, 1) % TOK
    length = new[PAIR : PAIR + STATS, :].astype(F32)[0:1, 0:1]
    attended = jnp.where(tok.astype(F32) < length, attended, 0.0)
    for g in range(GROUP):
        out[:, g * HEAD : (g + 1) * HEAD] = attended[:, g * TOK : (g + 1) * TOK].T.astype(BF16)


def finish(new, own, left, right):
    vmem = pl.BlockSpec(memory_space=pltpu.VMEM)
    return pl.pallas_call(
        finish_kernel,
        out_shape=jax.ShapeDtypeStruct((TOK, ROWS), BF16),
        in_specs=[vmem] * 4,
        out_specs=vmem,
        compiler_params=pltpu.CompilerParams(vmem_limit_bytes=MERGE_BYTES),
        cost_estimate=pl.CostEstimate(flops=8 * PART * ROWS, bytes_accessed=2**20, transcendentals=4 * ROWS),
    )(new, own, left, right)


def along_z(x, k):
    return lax.ppermute(x, "ctx", [(y * NZ + z, y * NZ + (z + k) % NZ) for y in range(NY) for z in range(NZ)])


def along_y(x, k):
    return lax.ppermute(x, "ctx", [(y * NZ + z, (y + k) % NY * NZ + z) for y in range(NY) for z in range(NZ)])


def along_x(x, k):
    return lax.ppermute(x, "tp", [(2 * i + c, 2 * ((i + k) % NX) + c) for i in range(NX) for c in range(2)])


def at(x, i):
    return lax.dynamic_index_in_dim(x, i, 0, keepdims=False)


def to_tiles(tile):
    pairs = []
    for y in range(NY):
        for z in range(NZ):
            for x in range(NX):
                for c in range(2):
                    source = (y * NZ + z) * 2 * NX + 2 * x + c
                    pairs.append((source, (x * NZ + z) * 2 * NX + 2 * y + c))
    return lax.ppermute(tile, ("ctx", "tp"), pairs)


def shards(
    queries,
    new_keys,
    new_values,
    store_keys,
    store_values,
    hit_blocks,
    hit_counts,
    new_lengths,
    out_weight,
):
    me = lax.axis_index("ctx")
    t = lax.axis_index("tp")
    y, z = me // NZ, me % NZ
    x, core = t // 2, t % 2

    blocks = jnp.concatenate([store_keys, jnp.swapaxes(store_values, 1, 2)], axis=1).reshape(STORE * PAIR, HEAD)
    lists = jnp.stack([hit_blocks.reshape(-1), jnp.pad(hit_counts[0], (0, 128 - hit_counts.shape[1]))])
    store = jnp.concatenate([blocks, jnp.pad(lists, ((0, STATS - 2), (0, 0))).astype(BF16)], axis=0)
    store_l, store_r = along_y(store, 1), along_y(store, -1)
    middle = STORE // 2 * PAIR
    second = [store_l[:middle], store_r[middle:]]
    far = [along_y(second[0], 1), along_y(second[1], -1)]

    def listed(x):
        return x[-STATS : 2 - STATS].astype(jnp.int32)

    hits = [lists, listed(store_l), listed(store_r), listed(far[1])]

    half = ROWS // 2
    q_up = [queries]
    q_down = [queries]
    for _ in range(3):
        q_up.append(along_z(q_up[-1], -1))
        q_down.append(along_z(q_down[-1], 1))
    down, up, _, _, out_weight = lax.optimization_barrier((q_down[3], q_up[3], *second, out_weight))
    q_far = [along_z(down[:, :half], 1), along_z(up[:, half:], -1)]
    weights = lax.all_gather(
        out_weight,
        "ctx",
        axis=0,
        tiled=False,
        axis_index_groups=[[yy * NZ + zz for yy in range(NY)] for zz in range(NZ)],
    )

    lengths = jnp.broadcast_to(new_lengths.astype(BF16)[:, None], (STATS, HEAD))
    new = jnp.concatenate([new_keys, new_values.T, lengths], axis=0)

    def number(*places):
        return jnp.stack([y * NZ + (z + d) % NZ for d in places]).astype(jnp.int32)

    run = functools.partial(attend, hits=hits, stores=[store, store_l, store_r, *far])
    (opposite,) = run(number(4), qs=q_far, n_halves=2)
    got_l, got_r = along_z(opposite[:, :half], 1), along_z(opposite[:, half:], -1)
    for d in (3, 2, 1):
        both = run(number(d, -d), qs=[q_up[d], q_down[d]], n_halves=1)
        to_right, to_left = relay(d == 3, both, got_l, got_r)
        got_l, got_r = along_z(to_right, 1), along_z(to_left, -1)
    own = run(number(0), qs=[queries], n_halves=1, new=(new,))
    head_out = finish(new, own, got_l, got_r)

    columns = out_weight.shape[1]
    partial = jnp.zeros((NY, NZ, TOK, columns), BF16)

    def project(partial, pieces, places):
        rows = jnp.concatenate(pieces, axis=0)
        part = jnp.einsum("rk,xkc->xrc", rows, weights, preferred_element_type=F32).astype(BF16)
        part = part.reshape(NY, len(pieces), TOK, columns)
        for i, place in enumerate(places):
            partial = lax.dynamic_update_slice(partial, part[:, i : i + 1], (0, (z + place) % NZ, 0, 0))
        return partial

    up = down = head_out
    pieces, places = [head_out], [0]
    for d in (1, 2, 3, 4):
        if d > 1:
            up, down, partial = lax.optimization_barrier((up, down, partial))
        if d < 4:
            next_up, next_down = along_z(up, -1), along_z(down, 1)
            arriving = [next_up, next_down], [d, -d]
        else:
            far_l, far_r = along_z(down[:, :half], 1), along_z(up[:, half:], -1)
            arriving = [jnp.concatenate([far_l, far_r], axis=1)], [4]
        partial = project(partial, pieces, places)
        up, down = next_up, next_down
        pieces, places = arriving
    partial = project(partial, pieces, places)

    def share(i):
        return lax.dynamic_slice_in_dim(partial, i * (NZ // 2), NZ // 2, 1)

    swapped = lax.ppermute(share(1 - core), "tp", [(i, i ^ 1) for i in range(2 * NX)])
    summed = share(core).astype(F32) + swapped.astype(F32)
    summed = summed.reshape(NY, NZ // 2 * TOK, columns)
    thin = summed.astype(BF16)
    total = at(summed, x)
    for k in range(1, NX):
        total = total + along_x(at(thin, (x + k) % NX), k).astype(F32)
    return to_tiles(total.astype(BF16))


def solution(mesh):
    return jax.shard_map(
        shards,
        mesh=mesh,
        in_specs=(
            P("ctx", "tp"),
            P("ctx", "tp"),
            P("ctx", "tp"),
            P("ctx", None, "tp"),
            P("ctx", None, "tp"),
            P("ctx", None, None),
            P("ctx", None),
            P("ctx"),
            P("tp", "ctx"),
        ),
        out_specs=P("tp", "ctx"),
        check_vma=False,
    )
```

```python
import functools

import jax
import jax.numpy as jnp
from jax import lax
from jax.experimental import pallas as pl
from jax.experimental.pallas import tpu as pltpu
from jax.sharding import PartitionSpec as P

HEAD = 128
BLOCK = 128
MOST = 4
TOK = 128
GROUP = 8
ROWS = GROUP * TOK
STORE = 16
NY = 4
NZ = 8
NX = 4
STATS = 16
PART = HEAD + STATS
PAIR = 2 * BLOCK
CHUNK = 8
TAILS = (2, 4, 8)
ROOM = STORE + CHUNK
NEG = -1e30
SCALE2 = 1.4426950408889634 * HEAD**-0.5
VMEM_BYTES = 24 * 1024 * 1024
MERGE_BYTES = 16 * 1024 * 1024
F32 = jnp.float32
BF16 = jnp.bfloat16


def heads_down(q):
    return jnp.concatenate([q[:, g * HEAD : (g + 1) * HEAD] for g in range(q.shape[1] // HEAD)], axis=0)


def scores(k, q):
    return lax.dot_general(k, q, (((1,), (1,)), ((), ())), preferred_element_type=F32)


def fold8(s):
    return jnp.max(s.reshape(s.shape[0] // 8, 8, s.shape[1]), axis=0)


def stat_rows(m, l):
    high = l.astype(BF16).astype(F32)
    row = lax.broadcasted_iota(jnp.int32, (STATS, m.shape[1]), 0)
    zero = jnp.zeros((STATS, m.shape[1]), F32)
    out = jnp.where(row == 0, m, zero)
    out = jnp.where(row == 1, high, out)
    return jnp.where(row == 2, l - high, out).astype(BF16)


def parts_of(x):
    x = x.astype(F32)
    m = x[HEAD : HEAD + 1]
    l = x[HEAD + 1 : HEAD + 2] + x[HEAD + 2 : HEAD + 3]
    return x[0:HEAD], m, l


def merge(parts):
    top = functools.reduce(jnp.maximum, [m for _, m, _ in parts])
    weights = [jnp.exp2(m - top) for _, m, _ in parts]
    o = sum(w * o for w, (o, _, _) in zip(weights, parts))
    l = sum(w * l for w, (_, _, l) in zip(weights, parts))
    return o, top, l


def take(refs, n):
    return refs[:n], refs[n:]


def attend_kernel(n_seqs, n_halves, with_new, *refs):
    (seq_ref,), refs = take(refs, 1)
    hits, refs = take(refs, NY)
    q_refs, refs = take(refs, n_seqs * n_halves)
    stores, refs = take(refs, NY + 1)
    new, refs = take(refs, int(with_new))
    out, kv, q_raw, q_scr, s_scr, m_scr, acc, places, sems, q_sems = refs

    row = 0
    loads = []
    for i, ref in enumerate(stores):
        size = STORE * PAIR // (1 if i < NY - 1 else 2)
        loads.append(pltpu.make_async_copy(ref.at[pl.ds(0, size), :], kv.at[pl.ds(row, size), :], sems.at[i]))
        row += size
    q_loads = []
    width = ROWS // n_halves
    for i, ref in enumerate(q_refs):
        n, h = i // n_halves, i % n_halves
        q_loads.append(pltpu.make_async_copy(ref, q_raw.at[n, h], q_sems.at[i]))
    for load in q_loads + loads:
        load.start()

    counts = []
    for n in range(n_seqs):
        for i in range(ROOM):
            places[n, i] = 0
        pos = jnp.int32(0)
        seq = seq_ref[n]
        for h, hit in enumerate(hits):
            count = hit[1, seq]
            for j in range(MOST):
                places[n, pos] = h * STORE + hit[0, seq * MOST + j]
                pos = pos + (j < count).astype(jnp.int32)
        places[n, ROOM] = pos

    for load in q_loads:
        load.wait()
    for n in range(n_seqs):
        for g in range(GROUP):
            h, at = divmod(g * HEAD, width)
            q_scr[n, g * TOK : (g + 1) * TOK, :] = q_raw[n, h, :, at : at + HEAD]
    for load in loads:
        load.wait()

    def one(n, carry):
        count = places[n, ROOM]
        full = count // CHUNK
        tail = count - full * CHUNK

        def each(step):
            lax.fori_loop(0, full, lambda i, c: (step(i * CHUNK, CHUNK, False), c)[1], 0)
            low = 0
            for size in TAILS:

                @pl.when((tail > low) & (tail <= size))
                def _(size=size):
                    step(full * CHUNK, size, True)

                low = size

        def rows_of(base, size, shift):
            first = [pl.multiple_of(places[n, base + i] * PAIR + shift, BLOCK) for i in range(size)]
            return [kv[pl.ds(at, BLOCK), :] for at in first]

        q = q_scr[n]
        m_scr[...] = jnp.full_like(m_scr, NEG)
        acc[...] = jnp.zeros_like(acc)

        def first(base, size, masked):
            s = scores(jnp.concatenate(rows_of(base, size, 0), axis=0), q)
            if masked:
                key = lax.broadcasted_iota(jnp.int32, s.shape, 0)
                s = jnp.where(key < tail * BLOCK, s, NEG)
            s_scr[pl.ds(base, size)] = s.reshape(size, BLOCK, ROWS)
            m_scr[...] = jnp.maximum(m_scr[...], fold8(s))

        each(first)
        if with_new:
            s = scores(new[0][0:BLOCK, :], q)
            key = lax.broadcasted_iota(jnp.int32, s.shape, 0)
            tok = lax.broadcasted_iota(jnp.int32, s.shape, 1) % TOK
            s = jnp.where(key <= tok, s, NEG)
            s_scr[STORE] = s
            m_scr[...] = jnp.maximum(m_scr[...], fold8(s))

        m = (jnp.max(m_scr[...], axis=0, keepdims=True) * SCALE2).astype(BF16).astype(F32)

        def weigh(s, v):
            p = jnp.exp2(s * SCALE2 - m).astype(BF16)
            v = jnp.concatenate([v, jnp.ones((STATS, v.shape[1]), BF16)], axis=0)
            acc[...] += jnp.dot(v, p, preferred_element_type=F32)

        def second(base, size, masked):
            s = s_scr[pl.ds(base, size)].reshape(size * BLOCK, ROWS)
            weigh(s, jnp.concatenate(rows_of(base, size, BLOCK), axis=1))

        each(second)
        if with_new:
            weigh(s_scr[STORE], new[0][BLOCK:PAIR, :])
        out[n, 0:HEAD, :] = acc[0:HEAD, :].astype(BF16)
        out[n, HEAD:PART, :] = stat_rows(m, acc[HEAD : HEAD + 1, :])
        return carry

    lax.fori_loop(0, n_seqs, one, 0)


def attend(seqs, hits, qs, n_halves, stores, new=()):
    n_seqs = len(qs) // n_halves
    smem = pl.BlockSpec(memory_space=pltpu.SMEM)
    vmem = pl.BlockSpec(memory_space=pltpu.VMEM)
    anywhere = pl.BlockSpec(memory_space=pl.ANY)
    work = n_seqs * 8
    return pl.pallas_call(
        functools.partial(attend_kernel, n_seqs, n_halves, len(new) > 0),
        out_shape=jax.ShapeDtypeStruct((n_seqs, PART, ROWS), BF16),
        in_specs=[smem] * (1 + NY) + [anywhere] * (len(qs) + len(stores)) + [vmem] * len(new),
        out_specs=vmem,
        scratch_shapes=[
            pltpu.VMEM((NY * STORE * PAIR, HEAD), BF16),
            pltpu.VMEM((n_seqs, n_halves, TOK, ROWS // n_halves), BF16),
            pltpu.VMEM((n_seqs, ROWS, HEAD), BF16),
            pltpu.VMEM((STORE + 1, BLOCK, ROWS), F32),
            pltpu.VMEM((8, ROWS), F32),
            pltpu.VMEM((PART, ROWS), F32),
            pltpu.SMEM((n_seqs, ROOM + 1), jnp.int32),
            pltpu.SemaphoreType.DMA((NY + 1,)),
            pltpu.SemaphoreType.DMA((len(qs),)),
        ],
        compiler_params=pltpu.CompilerParams(vmem_limit_bytes=VMEM_BYTES),
        cost_estimate=pl.CostEstimate(
            flops=work * 4 * BLOCK * ROWS * HEAD,
            bytes_accessed=5 * 2**20,
            transcendentals=work * BLOCK * ROWS,
        ),
    )(seqs, *hits, *qs, *stores, *new)


def relay_kernel(halves, own, got_a, got_b, out_a, out_b):
    half = ROWS // 2
    for n, (got, out) in enumerate(((got_a, out_a), (got_b, out_b))):
        cols = slice(0, ROWS)
        if halves:
            cols = slice(n * half, (n + 1) * half)
            rest = slice((1 - n) * half, (2 - n) * half)
            out[:, rest] = own[n, :, rest]
        o, m, l = merge([parts_of(own[n, :, cols]), parts_of(got[...])])
        out[0:HEAD, cols] = o.astype(BF16)
        out[HEAD:PART, cols] = stat_rows(m, l)


def relay(halves, own, got_a, got_b):
    vmem = pl.BlockSpec(memory_space=pltpu.VMEM)
    return pl.pallas_call(
        functools.partial(relay_kernel, halves),
        out_shape=[jax.ShapeDtypeStruct((PART, ROWS), BF16)] * 2,
        in_specs=[vmem] * 3,
        out_specs=[vmem] * 2,
        compiler_params=pltpu.CompilerParams(vmem_limit_bytes=MERGE_BYTES),
        cost_estimate=pl.CostEstimate(flops=8 * PART * ROWS, bytes_accessed=2 * 2**20, transcendentals=4 * ROWS),
    )(own, got_a, got_b)


def finish_kernel(new, own, left, right, out):
    o, _, l = merge([parts_of(own[0]), parts_of(left[...]), parts_of(right[...])])
    attended = o / l
    tok = lax.broadcasted_iota(jnp.int32, attended.shape, 1) % TOK
    length = new[PAIR : PAIR + STATS, :].astype(F32)[0:1, 0:1]
    attended = jnp.where(tok.astype(F32) < length, attended, 0.0)
    for g in range(GROUP):
        out[:, g * HEAD : (g + 1) * HEAD] = attended[:, g * TOK : (g + 1) * TOK].T.astype(BF16)


def finish(new, own, left, right):
    vmem = pl.BlockSpec(memory_space=pltpu.VMEM)
    return pl.pallas_call(
        finish_kernel,
        out_shape=jax.ShapeDtypeStruct((TOK, ROWS), BF16),
        in_specs=[vmem] * 4,
        out_specs=vmem,
        compiler_params=pltpu.CompilerParams(vmem_limit_bytes=MERGE_BYTES),
        cost_estimate=pl.CostEstimate(flops=8 * PART * ROWS, bytes_accessed=2**20, transcendentals=4 * ROWS),
    )(new, own, left, right)


def along_z(x, k):
    return lax.ppermute(x, "ctx", [(y * NZ + z, y * NZ + (z + k) % NZ) for y in range(NY) for z in range(NZ)])


def along_y(x, k):
    return lax.ppermute(x, "ctx", [(y * NZ + z, (y + k) % NY * NZ + z) for y in range(NY) for z in range(NZ)])


def along_x(x, k):
    return lax.ppermute(x, "tp", [(2 * i + c, 2 * ((i + k) % NX) + c) for i in range(NX) for c in range(2)])


def in_hbm(x):
    return pltpu.with_memory_space_constraint(x, pltpu.HBM)


def at(x, i):
    return lax.dynamic_index_in_dim(x, i, 0, keepdims=False)


def to_tiles(tile):
    pairs = []
    for y in range(NY):
        for z in range(NZ):
            for x in range(NX):
                for c in range(2):
                    source = (y * NZ + z) * 2 * NX + 2 * x + c
                    pairs.append((source, (x * NZ + z) * 2 * NX + 2 * y + c))
    return lax.ppermute(tile, ("ctx", "tp"), pairs)


def shards(
    queries,
    new_keys,
    new_values,
    store_keys,
    store_values,
    hit_blocks,
    hit_counts,
    new_lengths,
    out_weight,
):
    me = lax.axis_index("ctx")
    t = lax.axis_index("tp")
    y, z = me // NZ, me % NZ
    x, core = t // 2, t % 2

    blocks = jnp.concatenate([store_keys, jnp.swapaxes(store_values, 1, 2)], axis=1).reshape(STORE * PAIR, HEAD)
    lists = jnp.stack([hit_blocks.reshape(-1), jnp.pad(hit_counts[0], (0, 128 - hit_counts.shape[1]))])
    store = jnp.concatenate([blocks, jnp.pad(lists, ((0, STATS - 2), (0, 0))).astype(BF16)], axis=0)
    store_l, store_r = along_y(store, 1), along_y(store, -1)
    middle = STORE // 2 * PAIR
    second = [store_l[:middle], store_r[middle:]]
    far = [along_y(second[0], 1), along_y(second[1], -1)]

    def listed(x):
        return x[-STATS : 2 - STATS].astype(jnp.int32)

    hits = [lists, listed(store_l), listed(store_r), listed(far[1])]

    half = ROWS // 2
    q_up = [queries]
    q_down = [queries]
    for _ in range(3):
        q_up.append(along_z(q_up[-1], -1))
        q_down.append(along_z(q_down[-1], 1))
    down, up, _, _ = lax.optimization_barrier((q_down[3], q_up[3], *second))
    q_far = [along_z(down[:, :half], 1), along_z(up[:, half:], -1)]
    lengths = jnp.broadcast_to(new_lengths.astype(BF16)[:, None], (STATS, HEAD))
    new = jnp.concatenate([new_keys, new_values.T, lengths], axis=0)

    def number(*places):
        return jnp.stack([y * NZ + (z + d) % NZ for d in places]).astype(jnp.int32)

    far = [in_hbm(piece) for piece in far]
    store_r = in_hbm(store_r)
    run = functools.partial(attend, hits=hits, stores=[store, store_l, store_r, *far])
    (opposite,) = run(number(4), qs=q_far, n_halves=2)
    out_weight, _ = lax.optimization_barrier((out_weight, opposite))
    weights = lax.all_gather(
        out_weight,
        "ctx",
        axis=0,
        tiled=False,
        axis_index_groups=[[yy * NZ + zz for yy in range(NY)] for zz in range(NZ)],
    )

    got_l, got_r = along_z(opposite[:, :half], 1), along_z(opposite[:, half:], -1)
    for d in (3, 2, 1):
        both = run(number(d, -d), qs=[in_hbm(q_up[d]), in_hbm(q_down[d])], n_halves=1)
        to_right, to_left = relay(d == 3, both, got_l, got_r)
        got_l, got_r = along_z(to_right, 1), along_z(to_left, -1)
    own = run(number(0), qs=[in_hbm(queries)], n_halves=1, new=(new,))
    head_out = finish(new, own, got_l, got_r)

    columns = out_weight.shape[1]
    partial = jnp.zeros((NY, NZ, TOK, columns), BF16)

    def project(partial, pieces, places):
        rows = jnp.concatenate(pieces, axis=0)
        part = jnp.einsum("rk,xkc->xrc", rows, weights, preferred_element_type=F32).astype(BF16)
        part = part.reshape(NY, len(pieces), TOK, columns)
        for i, place in enumerate(places):
            partial = lax.dynamic_update_slice(partial, part[:, i : i + 1], (0, (z + place) % NZ, 0, 0))
        return partial

    up = down = head_out
    pieces, places = [head_out], [0]
    for d in (1, 2, 3, 4):
        if d > 1:
            up, down, partial = lax.optimization_barrier((up, down, partial))
        if d < 4:
            next_up, next_down = along_z(up, -1), along_z(down, 1)
            arriving = [next_up, next_down], [d, -d]
        else:
            far_l, far_r = along_z(down[:, :half], 1), along_z(up[:, half:], -1)
            arriving = [jnp.concatenate([far_l, far_r], axis=1)], [4]
        partial = project(partial, pieces, places)
        up, down = next_up, next_down
        pieces, places = arriving
    partial = project(partial, pieces, places)

    def share(i):
        return lax.dynamic_slice_in_dim(partial, i * (NZ // 2), NZ // 2, 1)

    swapped = lax.ppermute(share(1 - core), "tp", [(i, i ^ 1) for i in range(2 * NX)])
    summed = share(core).astype(F32) + swapped.astype(F32)
    summed = summed.reshape(NY, NZ // 2 * TOK, columns)
    thin = summed.astype(BF16)
    total = at(summed, x)
    for k in range(1, NX):
        total = total + along_x(at(thin, (x + k) % NX), k).astype(F32)
    return to_tiles(total.astype(BF16))


def solution(mesh):
    return jax.shard_map(
        shards,
        mesh=mesh,
        in_specs=(
            P("ctx", "tp"),
            P("ctx", "tp"),
            P("ctx", "tp"),
            P("ctx", None, "tp"),
            P("ctx", None, "tp"),
            P("ctx", None, None),
            P("ctx", None),
            P("ctx"),
            P("tp", "ctx"),
        ),
        out_specs=P("tp", "ctx"),
        check_vma=False,
    )
```

```python
import functools

import jax
import jax.numpy as jnp
from jax import lax
from jax.experimental import pallas as pl
from jax.experimental.pallas import tpu as pltpu
from jax.sharding import PartitionSpec as P

HEAD = 128
BLOCK = 128
MOST = 4
TOK = 128
GROUP = 8
ROWS = GROUP * TOK
STORE = 16
NY = 4
NZ = 8
NX = 4
STATS = 16
PART = HEAD + STATS
PAIR = 2 * BLOCK
CHUNK = 8
TAILS = (2, 4, 8)
ROOM = STORE + CHUNK
NEG = -1e30
SCALE2 = 1.4426950408889634 * HEAD**-0.5
VMEM_BYTES = 24 * 1024 * 1024
MERGE_BYTES = 16 * 1024 * 1024
F32 = jnp.float32
BF16 = jnp.bfloat16


def heads_down(q):
    return jnp.concatenate([q[:, g * HEAD : (g + 1) * HEAD] for g in range(q.shape[1] // HEAD)], axis=0)


def scores(k, q):
    return lax.dot_general(k, q, (((1,), (1,)), ((), ())), preferred_element_type=F32)


def fold8(s):
    return jnp.max(s.reshape(s.shape[0] // 8, 8, s.shape[1]), axis=0)


def stat_rows(m, l):
    high = l.astype(BF16).astype(F32)
    row = lax.broadcasted_iota(jnp.int32, (STATS, m.shape[1]), 0)
    zero = jnp.zeros((STATS, m.shape[1]), F32)
    out = jnp.where(row == 0, m, zero)
    out = jnp.where(row == 1, high, out)
    return jnp.where(row == 2, l - high, out).astype(BF16)


def parts_of(x):
    x = x.astype(F32)
    m = x[HEAD : HEAD + 1]
    l = x[HEAD + 1 : HEAD + 2] + x[HEAD + 2 : HEAD + 3]
    return x[0:HEAD], m, l


def merge(parts):
    top = functools.reduce(jnp.maximum, [m for _, m, _ in parts])
    weights = [jnp.exp2(m - top) for _, m, _ in parts]
    o = sum(w * o for w, (o, _, _) in zip(weights, parts))
    l = sum(w * l for w, (_, _, l) in zip(weights, parts))
    return o, top, l


def take(refs, n):
    return refs[:n], refs[n:]


def attend_kernel(offsets, n_halves, with_new, *refs):
    n_seqs = len(offsets)
    (where,), refs = take(refs, 1)
    hits, refs = take(refs, NY)
    q_refs, refs = take(refs, n_seqs * n_halves)
    stores, refs = take(refs, NY + 1)
    new, refs = take(refs, int(with_new))
    out, kv, q_raw, q_scr, s_scr, m_scr, acc, places, sems, q_sems = refs

    row = 0
    loads = []
    for i, ref in enumerate(stores):
        size = STORE * PAIR // (1 if i < NY - 1 else 2)
        loads.append(pltpu.make_async_copy(ref.at[pl.ds(0, size), :], kv.at[pl.ds(row, size), :], sems.at[i]))
        row += size
    q_loads = []
    width = ROWS // n_halves
    for i, ref in enumerate(q_refs):
        n, h = i // n_halves, i % n_halves
        q_loads.append(pltpu.make_async_copy(ref, q_raw.at[n, h], q_sems.at[i]))
    for load in q_loads + loads:
        load.start()

    counts = []
    for n in range(n_seqs):
        for i in range(ROOM):
            places[n, i] = 0
        pos = jnp.int32(0)
        seq = where[0] * NZ + lax.rem(where[1] + (offsets[n] + NZ), NZ)
        for h, hit in enumerate(hits):
            count = hit[1, seq]
            for j in range(MOST):
                places[n, pos] = h * STORE + hit[0, seq * MOST + j]
                pos = pos + (j < count).astype(jnp.int32)
        places[n, ROOM] = pos

    for load in q_loads:
        load.wait()
    for n in range(n_seqs):
        for g in range(GROUP):
            h, at = divmod(g * HEAD, width)
            q_scr[n, g * TOK : (g + 1) * TOK, :] = q_raw[n, h, :, at : at + HEAD]
    for load in loads:
        load.wait()

    def one(n, carry):
        count = places[n, ROOM]
        full = count // CHUNK
        tail = count - full * CHUNK

        def each(step):
            lax.fori_loop(0, full, lambda i, c: (step(i * CHUNK, CHUNK, False), c)[1], 0)
            low = 0
            for size in TAILS:

                @pl.when((tail > low) & (tail <= size))
                def _(size=size):
                    step(full * CHUNK, size, True)

                low = size

        def rows_of(base, size, shift):
            first = [pl.multiple_of(places[n, base + i] * PAIR + shift, BLOCK) for i in range(size)]
            return [kv[pl.ds(at, BLOCK), :] for at in first]

        q = q_scr[n]
        m_scr[...] = jnp.full_like(m_scr, NEG)
        acc[...] = jnp.zeros_like(acc)

        def first(base, size, masked):
            s = scores(jnp.concatenate(rows_of(base, size, 0), axis=0), q)
            if masked:
                key = lax.broadcasted_iota(jnp.int32, s.shape, 0)
                s = jnp.where(key < tail * BLOCK, s, NEG)
            s_scr[pl.ds(base, size)] = s.reshape(size, BLOCK, ROWS)
            m_scr[...] = jnp.maximum(m_scr[...], fold8(s))

        each(first)
        if with_new:
            s = scores(new[0][0:BLOCK, :], q)
            key = lax.broadcasted_iota(jnp.int32, s.shape, 0)
            tok = lax.broadcasted_iota(jnp.int32, s.shape, 1) % TOK
            s = jnp.where(key <= tok, s, NEG)
            s_scr[STORE] = s
            m_scr[...] = jnp.maximum(m_scr[...], fold8(s))

        m = (jnp.max(m_scr[...], axis=0, keepdims=True) * SCALE2).astype(BF16).astype(F32)

        def weigh(s, v):
            p = jnp.exp2(s * SCALE2 - m).astype(BF16)
            v = jnp.concatenate([v, jnp.ones((STATS, v.shape[1]), BF16)], axis=0)
            acc[...] += jnp.dot(v, p, preferred_element_type=F32)

        def second(base, size, masked):
            s = s_scr[pl.ds(base, size)].reshape(size * BLOCK, ROWS)
            weigh(s, jnp.concatenate(rows_of(base, size, BLOCK), axis=1))

        each(second)
        if with_new:
            weigh(s_scr[STORE], new[0][BLOCK:PAIR, :])
        out[n, 0:HEAD, :] = acc[0:HEAD, :].astype(BF16)
        out[n, HEAD:PART, :] = stat_rows(m, acc[HEAD : HEAD + 1, :])
        return carry

    lax.fori_loop(0, n_seqs, one, 0)


def attend(offsets, where, hits, qs, n_halves, stores, new=()):
    n_seqs = len(offsets)
    smem = pl.BlockSpec(memory_space=pltpu.SMEM)
    vmem = pl.BlockSpec(memory_space=pltpu.VMEM)
    anywhere = pl.BlockSpec(memory_space=pl.ANY)
    work = n_seqs * 8
    return pl.pallas_call(
        functools.partial(attend_kernel, offsets, n_halves, len(new) > 0),
        out_shape=jax.ShapeDtypeStruct((n_seqs, PART, ROWS), BF16),
        in_specs=[smem] * (1 + NY) + [anywhere] * (len(qs) + len(stores)) + [vmem] * len(new),
        out_specs=vmem,
        scratch_shapes=[
            pltpu.VMEM((NY * STORE * PAIR, HEAD), BF16),
            pltpu.VMEM((n_seqs, n_halves, TOK, ROWS // n_halves), BF16),
            pltpu.VMEM((n_seqs, ROWS, HEAD), BF16),
            pltpu.VMEM((STORE + 1, BLOCK, ROWS), F32),
            pltpu.VMEM((8, ROWS), F32),
            pltpu.VMEM((PART, ROWS), F32),
            pltpu.SMEM((n_seqs, ROOM + 1), jnp.int32),
            pltpu.SemaphoreType.DMA((NY + 1,)),
            pltpu.SemaphoreType.DMA((len(qs),)),
        ],
        compiler_params=pltpu.CompilerParams(vmem_limit_bytes=VMEM_BYTES),
        cost_estimate=pl.CostEstimate(
            flops=work * 4 * BLOCK * ROWS * HEAD,
            bytes_accessed=5 * 2**20,
            transcendentals=work * BLOCK * ROWS,
        ),
    )(where, *hits, *qs, *stores, *new)


def pack_kernel(keys, values, lists, out):
    for b in range(STORE):
        out[b * PAIR : b * PAIR + BLOCK, :] = keys[b]
        out[b * PAIR + BLOCK : (b + 1) * PAIR, :] = values[b].T
    out[STORE * PAIR :, :] = lists[...]


def pack(keys, values, lists):
    vmem = pl.BlockSpec(memory_space=pltpu.VMEM)
    return pl.pallas_call(
        pack_kernel,
        out_shape=jax.ShapeDtypeStruct((STORE * PAIR + STATS, HEAD), BF16),
        in_specs=[vmem] * 3,
        out_specs=vmem,
        compiler_params=pltpu.CompilerParams(vmem_limit_bytes=MERGE_BYTES),
        cost_estimate=pl.CostEstimate(flops=0, bytes_accessed=2 * 2**20, transcendentals=0),
    )(keys, values, lists)


def relay_kernel(halves, own, got_a, got_b, out_a, out_b):
    half = ROWS // 2
    for n, (got, out) in enumerate(((got_a, out_a), (got_b, out_b))):
        cols = slice(0, ROWS)
        if halves:
            cols = slice(n * half, (n + 1) * half)
            rest = slice((1 - n) * half, (2 - n) * half)
            out[:, rest] = own[n, :, rest]
        o, m, l = merge([parts_of(own[n, :, cols]), parts_of(got[...])])
        out[0:HEAD, cols] = o.astype(BF16)
        out[HEAD:PART, cols] = stat_rows(m, l)


def relay(halves, own, got_a, got_b):
    vmem = pl.BlockSpec(memory_space=pltpu.VMEM)
    return pl.pallas_call(
        functools.partial(relay_kernel, halves),
        out_shape=[jax.ShapeDtypeStruct((PART, ROWS), BF16)] * 2,
        in_specs=[vmem] * 3,
        out_specs=[vmem] * 2,
        compiler_params=pltpu.CompilerParams(vmem_limit_bytes=MERGE_BYTES),
        cost_estimate=pl.CostEstimate(flops=8 * PART * ROWS, bytes_accessed=2 * 2**20, transcendentals=4 * ROWS),
    )(own, got_a, got_b)


def finish_kernel(new, own, left, right, out):
    o, _, l = merge([parts_of(own[0]), parts_of(left[...]), parts_of(right[...])])
    attended = o / l
    tok = lax.broadcasted_iota(jnp.int32, attended.shape, 1) % TOK
    length = new[PAIR : PAIR + STATS, :].astype(F32)[0:1, 0:1]
    attended = jnp.where(tok.astype(F32) < length, attended, 0.0)
    for g in range(GROUP):
        out[:, g * HEAD : (g + 1) * HEAD] = attended[:, g * TOK : (g + 1) * TOK].T.astype(BF16)


def finish(new, own, left, right):
    vmem = pl.BlockSpec(memory_space=pltpu.VMEM)
    return pl.pallas_call(
        finish_kernel,
        out_shape=jax.ShapeDtypeStruct((TOK, ROWS), BF16),
        in_specs=[vmem] * 4,
        out_specs=vmem,
        compiler_params=pltpu.CompilerParams(vmem_limit_bytes=MERGE_BYTES),
        cost_estimate=pl.CostEstimate(flops=8 * PART * ROWS, bytes_accessed=2**20, transcendentals=4 * ROWS),
    )(new, own, left, right)


def along_z(x, k):
    return lax.ppermute(x, "ctx", [(y * NZ + z, y * NZ + (z + k) % NZ) for y in range(NY) for z in range(NZ)])


def along_y(x, k):
    return lax.ppermute(x, "ctx", [(y * NZ + z, (y + k) % NY * NZ + z) for y in range(NY) for z in range(NZ)])


def along_x(x, k):
    return lax.ppermute(x, "tp", [(2 * i + c, 2 * ((i + k) % NX) + c) for i in range(NX) for c in range(2)])


def in_hbm(x):
    return pltpu.with_memory_space_constraint(x, pltpu.HBM)


def at(x, i):
    return lax.dynamic_index_in_dim(x, i, 0, keepdims=False)


def to_tiles(tile):
    pairs = []
    for y in range(NY):
        for z in range(NZ):
            for x in range(NX):
                for c in range(2):
                    source = (y * NZ + z) * 2 * NX + 2 * x + c
                    pairs.append((source, (x * NZ + z) * 2 * NX + 2 * y + c))
    return lax.ppermute(tile, ("ctx", "tp"), pairs)


def shards(
    queries,
    new_keys,
    new_values,
    store_keys,
    store_values,
    hit_blocks,
    hit_counts,
    new_lengths,
    out_weight,
):
    me = lax.axis_index("ctx")
    t = lax.axis_index("tp")
    y, z = me // NZ, me % NZ
    x, core = t // 2, t % 2

    lists = jnp.stack([hit_blocks.reshape(-1), jnp.pad(hit_counts[0], (0, 128 - hit_counts.shape[1]))])
    store = pack(store_keys, store_values, jnp.pad(lists, ((0, STATS - 2), (0, 0))).astype(BF16))
    store_l, store_r = along_y(store, 1), along_y(store, -1)
    middle = STORE // 2 * PAIR
    second = [store_l[:middle], store_r[middle:]]
    far = [along_y(second[0], 1), along_y(second[1], -1)]

    def listed(x):
        return x[-STATS : 2 - STATS].astype(jnp.int32)

    hits = [lists, listed(store_l), listed(store_r), listed(far[1])]

    half = ROWS // 2
    q_up = [queries]
    q_down = [queries]
    for _ in range(3):
        q_up.append(along_z(q_up[-1], -1))
        q_down.append(along_z(q_down[-1], 1))
    down, up, _, _ = lax.optimization_barrier((q_down[3], q_up[3], *second))
    q_far = [along_z(down[:, :half], 1), along_z(up[:, half:], -1)]
    lengths = jnp.broadcast_to(new_lengths.astype(BF16)[:, None], (STATS, HEAD))
    new = jnp.concatenate([new_keys, new_values.T, lengths], axis=0)

    far = [in_hbm(piece) for piece in far]
    store_r = in_hbm(store_r)
    where = jnp.stack([y, z]).astype(jnp.int32)
    run = functools.partial(attend, where=where, hits=hits, stores=[store, store_l, store_r, *far])
    (opposite,) = run((4,), qs=q_far, n_halves=2)
    out_weight, _ = lax.optimization_barrier((out_weight, opposite))
    weights = lax.all_gather(
        out_weight,
        "ctx",
        axis=0,
        tiled=False,
        axis_index_groups=[[yy * NZ + zz for yy in range(NY)] for zz in range(NZ)],
    )

    got_l, got_r = along_z(opposite[:, :half], 1), along_z(opposite[:, half:], -1)
    for d in (3, 2, 1):
        both = run((d, -d), qs=[in_hbm(q_up[d]), in_hbm(q_down[d])], n_halves=1)
        to_right, to_left = relay(d == 3, both, got_l, got_r)
        got_l, got_r = along_z(to_right, 1), along_z(to_left, -1)
    own = run((0,), qs=[in_hbm(queries)], n_halves=1, new=(new,))
    head_out = finish(new, own, got_l, got_r)

    columns = out_weight.shape[1]
    partial = jnp.zeros((NY, NZ, TOK, columns), BF16)

    def project(partial, pieces, places):
        rows = jnp.concatenate(pieces, axis=0)
        part = jnp.einsum("rk,xkc->xrc", rows, weights, preferred_element_type=F32).astype(BF16)
        part = part.reshape(NY, len(pieces), TOK, columns)
        for i, place in enumerate(places):
            partial = lax.dynamic_update_slice(partial, part[:, i : i + 1], (0, (z + place) % NZ, 0, 0))
        return partial

    up = down = head_out
    pieces, places = [head_out], [0]
    for d in (1, 2, 3, 4):
        if d > 1:
            up, down, partial = lax.optimization_barrier((up, down, partial))
        if d < 4:
            next_up, next_down = along_z(up, -1), along_z(down, 1)
            arriving = [next_up, next_down], [d, -d]
        else:
            far_l, far_r = along_z(down[:, :half], 1), along_z(up[:, half:], -1)
            arriving = [jnp.concatenate([far_l, far_r], axis=1)], [4]
        partial = project(partial, pieces, places)
        up, down = next_up, next_down
        pieces, places = arriving
    partial = project(partial, pieces, places)

    def share(i):
        return lax.dynamic_slice_in_dim(partial, i * (NZ // 2), NZ // 2, 1)

    swapped = lax.ppermute(share(1 - core), "tp", [(i, i ^ 1) for i in range(2 * NX)])
    summed = share(core).astype(F32) + swapped.astype(F32)
    summed = summed.reshape(NY, NZ // 2 * TOK, columns)
    thin = summed.astype(BF16)
    total = at(summed, x)
    for k in range(1, NX):
        total = total + along_x(at(thin, (x + k) % NX), k).astype(F32)
    return to_tiles(total.astype(BF16))


def solution(mesh):
    return jax.shard_map(
        shards,
        mesh=mesh,
        in_specs=(
            P("ctx", "tp"),
            P("ctx", "tp"),
            P("ctx", "tp"),
            P("ctx", None, "tp"),
            P("ctx", None, "tp"),
            P("ctx", None, None),
            P("ctx", None),
            P("ctx"),
            P("tp", "ctx"),
        ),
        out_specs=P("tp", "ctx"),
        check_vma=False,
    )
```

```python
import functools

import jax
import jax.numpy as jnp
from jax import lax
from jax.experimental import pallas as pl
from jax.experimental.pallas import tpu as pltpu
from jax.sharding import PartitionSpec as P

HEAD = 128
BLOCK = 128
MOST = 4
TOK = 128
GROUP = 8
ROWS = GROUP * TOK
STORE = 16
NY = 4
NZ = 8
NX = 4
STATS = 16
PART = HEAD + STATS
PAIR = 2 * BLOCK
CHUNK = 8
TAILS = (2, 4, 8)
ROOM = STORE + CHUNK
NEG = -1e30
SCALE2 = 1.4426950408889634 * HEAD**-0.5
VMEM_BYTES = 24 * 1024 * 1024
MERGE_BYTES = 16 * 1024 * 1024
F32 = jnp.float32
BF16 = jnp.bfloat16


def heads_down(q):
    return jnp.concatenate([q[:, g * HEAD : (g + 1) * HEAD] for g in range(q.shape[1] // HEAD)], axis=0)


def scores(k, q):
    return lax.dot_general(k, q, (((1,), (1,)), ((), ())), preferred_element_type=F32)


def fold8(s):
    return jnp.max(s.reshape(s.shape[0] // 8, 8, s.shape[1]), axis=0)


def stat_rows(m, l):
    high = l.astype(BF16).astype(F32)
    row = lax.broadcasted_iota(jnp.int32, (STATS, m.shape[1]), 0)
    zero = jnp.zeros((STATS, m.shape[1]), F32)
    out = jnp.where(row == 0, m, zero)
    out = jnp.where(row == 1, high, out)
    return jnp.where(row == 2, l - high, out).astype(BF16)


def parts_of(x):
    x = x.astype(F32)
    m = x[HEAD : HEAD + 1]
    l = x[HEAD + 1 : HEAD + 2] + x[HEAD + 2 : HEAD + 3]
    return x[0:HEAD], m, l


def merge(parts):
    top = functools.reduce(jnp.maximum, [m for _, m, _ in parts])
    weights = [jnp.exp2(m - top) for _, m, _ in parts]
    o = sum(w * o for w, (o, _, _) in zip(weights, parts))
    l = sum(w * l for w, (_, _, l) in zip(weights, parts))
    return o, top, l


def take(refs, n):
    return refs[:n], refs[n:]


def attend_kernel(offsets, n_halves, with_new, *refs):
    n_seqs = len(offsets)
    (where,), refs = take(refs, 1)
    hits, refs = take(refs, NY)
    q_refs, refs = take(refs, n_seqs * n_halves)
    stores, refs = take(refs, NY + 1)
    new, refs = take(refs, int(with_new))
    out, kv, q_raw, q_scr, s_scr, m_scr, acc, places, sems, q_sems = refs

    row = 0
    loads = []
    for i, ref in enumerate(stores):
        size = STORE * PAIR // (1 if i < NY - 1 else 2)
        loads.append(pltpu.make_async_copy(ref.at[pl.ds(0, size), :], kv.at[pl.ds(row, size), :], sems.at[i]))
        row += size
    q_loads = []
    width = ROWS // n_halves
    for i, ref in enumerate(q_refs):
        n, h = i // n_halves, i % n_halves
        q_loads.append(pltpu.make_async_copy(ref, q_raw.at[n, h], q_sems.at[i]))
    for load in q_loads + loads:
        load.start()

    counts = []
    for n in range(n_seqs):
        for i in range(ROOM):
            places[n, i] = 0
        pos = jnp.int32(0)
        seq = where[0] * NZ + lax.rem(where[1] + (offsets[n] + NZ), NZ)
        for h, hit in enumerate(hits):
            count = hit[1, seq]
            for j in range(MOST):
                places[n, pos] = h * STORE + hit[0, seq * MOST + j]
                pos = pos + (j < count).astype(jnp.int32)
        places[n, ROOM] = pos

    for load in q_loads:
        load.wait()
    for n in range(n_seqs):
        for g in range(GROUP):
            h, at = divmod(g * HEAD, width)
            q_scr[n, g * TOK : (g + 1) * TOK, :] = q_raw[n, h, :, at : at + HEAD]
    for load in loads:
        load.wait()

    def one(n, carry):
        count = places[n, ROOM]
        full = count // CHUNK
        tail = count - full * CHUNK

        def each(step):
            lax.fori_loop(0, full, lambda i, c: (step(i * CHUNK, CHUNK, False), c)[1], 0)
            low = 0
            for size in TAILS:

                @pl.when((tail > low) & (tail <= size))
                def _(size=size):
                    step(full * CHUNK, size, True)

                low = size

        def rows_of(base, size, shift):
            first = [pl.multiple_of(places[n, base + i] * PAIR + shift, BLOCK) for i in range(size)]
            return [kv[pl.ds(at, BLOCK), :] for at in first]

        q = q_scr[n]
        m_scr[...] = jnp.full_like(m_scr, NEG)
        acc[...] = jnp.zeros_like(acc)

        def first(base, size, masked):
            s = scores(jnp.concatenate(rows_of(base, size, 0), axis=0), q)
            if masked:
                key = lax.broadcasted_iota(jnp.int32, s.shape, 0)
                s = jnp.where(key < tail * BLOCK, s, NEG)
            s_scr[pl.ds(base, size)] = s.reshape(size, BLOCK, ROWS)
            m_scr[...] = jnp.maximum(m_scr[...], fold8(s))

        each(first)
        if with_new:
            s = scores(new[0][0:BLOCK, :], q)
            key = lax.broadcasted_iota(jnp.int32, s.shape, 0)
            tok = lax.broadcasted_iota(jnp.int32, s.shape, 1) % TOK
            s = jnp.where(key <= tok, s, NEG)
            s_scr[STORE] = s
            m_scr[...] = jnp.maximum(m_scr[...], fold8(s))

        m = (jnp.max(m_scr[...], axis=0, keepdims=True) * SCALE2).astype(BF16).astype(F32)

        def weigh(s, v):
            p = jnp.exp2(s * SCALE2 - m).astype(BF16)
            v = jnp.concatenate([v, jnp.ones((STATS, v.shape[1]), BF16)], axis=0)
            acc[...] += jnp.dot(v, p, preferred_element_type=F32)

        def second(base, size, masked):
            s = s_scr[pl.ds(base, size)].reshape(size * BLOCK, ROWS)
            weigh(s, jnp.concatenate(rows_of(base, size, BLOCK), axis=1))

        each(second)
        if with_new:
            weigh(s_scr[STORE], new[0][BLOCK:PAIR, :])
        out[n, 0:HEAD, :] = acc[0:HEAD, :].astype(BF16)
        out[n, HEAD:PART, :] = stat_rows(m, acc[HEAD : HEAD + 1, :])
        return carry

    lax.fori_loop(0, n_seqs, one, 0)


def attend(offsets, where, hits, qs, n_halves, stores, new=()):
    n_seqs = len(offsets)
    smem = pl.BlockSpec(memory_space=pltpu.SMEM)
    vmem = pl.BlockSpec(memory_space=pltpu.VMEM)
    anywhere = pl.BlockSpec(memory_space=pl.ANY)
    work = n_seqs * 8
    return pl.pallas_call(
        functools.partial(attend_kernel, offsets, n_halves, len(new) > 0),
        out_shape=jax.ShapeDtypeStruct((n_seqs, PART, ROWS), BF16),
        in_specs=[smem] * (1 + NY) + [anywhere] * (len(qs) + len(stores)) + [vmem] * len(new),
        out_specs=vmem,
        scratch_shapes=[
            pltpu.VMEM((NY * STORE * PAIR, HEAD), BF16),
            pltpu.VMEM((n_seqs, n_halves, TOK, ROWS // n_halves), BF16),
            pltpu.VMEM((n_seqs, ROWS, HEAD), BF16),
            pltpu.VMEM((STORE + 1, BLOCK, ROWS), F32),
            pltpu.VMEM((8, ROWS), F32),
            pltpu.VMEM((PART, ROWS), F32),
            pltpu.SMEM((n_seqs, ROOM + 1), jnp.int32),
            pltpu.SemaphoreType.DMA((NY + 1,)),
            pltpu.SemaphoreType.DMA((len(qs),)),
        ],
        compiler_params=pltpu.CompilerParams(vmem_limit_bytes=VMEM_BYTES),
        cost_estimate=pl.CostEstimate(
            flops=work * 4 * BLOCK * ROWS * HEAD,
            bytes_accessed=5 * 2**20,
            transcendentals=work * BLOCK * ROWS,
        ),
    )(where, *hits, *qs, *stores, *new)


def pack_kernel(keys, values, lists, out):
    for b in range(STORE):
        out[b * PAIR : b * PAIR + BLOCK, :] = keys[b]
        out[b * PAIR + BLOCK : (b + 1) * PAIR, :] = values[b].T
    out[STORE * PAIR :, :] = lists[...]


def pack(keys, values, lists):
    vmem = pl.BlockSpec(memory_space=pltpu.VMEM)
    return pl.pallas_call(
        pack_kernel,
        out_shape=jax.ShapeDtypeStruct((STORE * PAIR + STATS, HEAD), BF16),
        in_specs=[vmem] * 3,
        out_specs=vmem,
        compiler_params=pltpu.CompilerParams(vmem_limit_bytes=MERGE_BYTES),
        cost_estimate=pl.CostEstimate(flops=0, bytes_accessed=2 * 2**20, transcendentals=0),
    )(keys, values, lists)


def relay_kernel(halves, own, got_a, got_b, out_a, out_b):
    half = ROWS // 2
    for n, (got, out) in enumerate(((got_a, out_a), (got_b, out_b))):
        cols = slice(0, ROWS)
        if halves:
            cols = slice(n * half, (n + 1) * half)
            rest = slice((1 - n) * half, (2 - n) * half)
            out[:, rest] = own[n, :, rest]
        o, m, l = merge([parts_of(own[n, :, cols]), parts_of(got[...])])
        out[0:HEAD, cols] = o.astype(BF16)
        out[HEAD:PART, cols] = stat_rows(m, l)


def relay(halves, own, got_a, got_b):
    vmem = pl.BlockSpec(memory_space=pltpu.VMEM)
    return pl.pallas_call(
        functools.partial(relay_kernel, halves),
        out_shape=[jax.ShapeDtypeStruct((PART, ROWS), BF16)] * 2,
        in_specs=[vmem] * 3,
        out_specs=[vmem] * 2,
        compiler_params=pltpu.CompilerParams(vmem_limit_bytes=MERGE_BYTES),
        cost_estimate=pl.CostEstimate(flops=8 * PART * ROWS, bytes_accessed=2 * 2**20, transcendentals=4 * ROWS),
    )(own, got_a, got_b)


def finish_kernel(new, own, left, right, out):
    o, _, l = merge([parts_of(own[0]), parts_of(left[...]), parts_of(right[...])])
    attended = o / l
    tok = lax.broadcasted_iota(jnp.int32, attended.shape, 1) % TOK
    length = new[PAIR : PAIR + STATS, :].astype(F32)[0:1, 0:1]
    attended = jnp.where(tok.astype(F32) < length, attended, 0.0)
    for g in range(GROUP):
        out[:, g * HEAD : (g + 1) * HEAD] = attended[:, g * TOK : (g + 1) * TOK].T.astype(BF16)


def finish(new, own, left, right):
    vmem = pl.BlockSpec(memory_space=pltpu.VMEM)
    return pl.pallas_call(
        finish_kernel,
        out_shape=jax.ShapeDtypeStruct((TOK, ROWS), BF16),
        in_specs=[vmem] * 4,
        out_specs=vmem,
        compiler_params=pltpu.CompilerParams(vmem_limit_bytes=MERGE_BYTES),
        cost_estimate=pl.CostEstimate(flops=8 * PART * ROWS, bytes_accessed=2**20, transcendentals=4 * ROWS),
    )(new, own, left, right)


def along_z(x, k):
    return lax.ppermute(x, "ctx", [(y * NZ + z, y * NZ + (z + k) % NZ) for y in range(NY) for z in range(NZ)])


def along_y(x, k):
    return lax.ppermute(x, "ctx", [(y * NZ + z, (y + k) % NY * NZ + z) for y in range(NY) for z in range(NZ)])


def along_x(x, k):
    return lax.ppermute(x, "tp", [(2 * i + c, 2 * ((i + k) % NX) + c) for i in range(NX) for c in range(2)])


def in_hbm(x):
    return pltpu.with_memory_space_constraint(x, pltpu.HBM)


def at(x, i):
    return lax.dynamic_index_in_dim(x, i, 0, keepdims=False)


def to_tiles(tile):
    pairs = []
    for y in range(NY):
        for z in range(NZ):
            for x in range(NX):
                for c in range(2):
                    source = (y * NZ + z) * 2 * NX + 2 * x + c
                    pairs.append((source, (x * NZ + z) * 2 * NX + 2 * y + c))
    return lax.ppermute(tile, ("ctx", "tp"), pairs)


def shards(
    queries,
    new_keys,
    new_values,
    store_keys,
    store_values,
    hit_blocks,
    hit_counts,
    new_lengths,
    out_weight,
):
    me = lax.axis_index("ctx")
    t = lax.axis_index("tp")
    y, z = me // NZ, me % NZ
    x, core = t // 2, t % 2

    lists = jnp.stack([hit_blocks.reshape(-1), jnp.pad(hit_counts[0], (0, 128 - hit_counts.shape[1]))])
    store = pack(store_keys, store_values, jnp.pad(lists, ((0, STATS - 2), (0, 0))).astype(BF16))
    store_l, store_r = along_y(store, 1), along_y(store, -1)
    middle = STORE // 2 * PAIR
    second = [store_l[:middle], store_r[middle:]]
    far = [along_y(second[0], 1), along_y(second[1], -1)]

    def listed(x):
        return x[-STATS : 2 - STATS].astype(jnp.int32)

    hits = [lists, listed(store_l), listed(store_r), along_y(lists, 2)]

    half = ROWS // 2
    q_up = [queries]
    q_down = [queries]
    for _ in range(3):
        q_up.append(along_z(q_up[-1], -1))
        q_down.append(along_z(q_down[-1], 1))
    down, up, _, _ = lax.optimization_barrier((q_down[3], q_up[3], *second))
    q_far = [along_z(down[:, :half], 1), along_z(up[:, half:], -1)]
    lengths = jnp.broadcast_to(new_lengths.astype(BF16)[:, None], (STATS, HEAD))
    new = jnp.concatenate([new_keys, new_values.T, lengths], axis=0)

    where = jnp.stack([y, z]).astype(jnp.int32)
    near = [store, store_l, store_r, *far]
    (opposite,) = attend((4,), where, hits, q_far, 2, near)
    far = [in_hbm(piece) for piece in far]
    store_r = in_hbm(store_r)
    run = functools.partial(attend, where=where, hits=hits, stores=[store, store_l, store_r, *far])
    out_weight, _ = lax.optimization_barrier((out_weight, opposite))
    weights = lax.all_gather(
        out_weight,
        "ctx",
        axis=0,
        tiled=False,
        axis_index_groups=[[yy * NZ + zz for yy in range(NY)] for zz in range(NZ)],
    )

    got_l, got_r = along_z(opposite[:, :half], 1), along_z(opposite[:, half:], -1)
    for d in (3, 2, 1):
        both = run((d, -d), qs=[in_hbm(q_up[d]), in_hbm(q_down[d])], n_halves=1)
        to_right, to_left = relay(d == 3, both, got_l, got_r)
        got_l, got_r = along_z(to_right, 1), along_z(to_left, -1)
    own = run((0,), qs=[in_hbm(queries)], n_halves=1, new=(new,))
    head_out = finish(new, own, got_l, got_r)

    columns = out_weight.shape[1]
    partial = jnp.zeros((NY, NZ, TOK, columns), BF16)

    def project(partial, pieces, places):
        rows = jnp.concatenate(pieces, axis=0)
        part = jnp.einsum("rk,xkc->xrc", rows, weights, preferred_element_type=F32).astype(BF16)
        part = part.reshape(NY, len(pieces), TOK, columns)
        for i, place in enumerate(places):
            partial = lax.dynamic_update_slice(partial, part[:, i : i + 1], (0, (z + place) % NZ, 0, 0))
        return partial

    up = down = head_out
    pieces, places = [head_out], [0]
    for d in (1, 2, 3, 4):
        if d > 1:
            up, down, partial = lax.optimization_barrier((up, down, partial))
        if d < 4:
            next_up, next_down = along_z(up, -1), along_z(down, 1)
            arriving = [next_up, next_down], [d, -d]
        else:
            far_l, far_r = along_z(down[:, :half], 1), along_z(up[:, half:], -1)
            arriving = [jnp.concatenate([far_l, far_r], axis=1)], [4]
        partial = project(partial, pieces, places)
        up, down = next_up, next_down
        pieces, places = arriving
    partial = project(partial, pieces, places)

    def share(i):
        return lax.dynamic_slice_in_dim(partial, i * (NZ // 2), NZ // 2, 1)

    swapped = lax.ppermute(share(1 - core), "tp", [(i, i ^ 1) for i in range(2 * NX)])
    summed = share(core).astype(F32) + swapped.astype(F32)
    summed = summed.reshape(NY, NZ // 2 * TOK, columns)
    thin = summed.astype(BF16)
    total = at(summed, x)
    for k in range(1, NX):
        total = total + along_x(at(thin, (x + k) % NX), k).astype(F32)
    return to_tiles(total.astype(BF16))


def solution(mesh):
    return jax.shard_map(
        shards,
        mesh=mesh,
        in_specs=(
            P("ctx", "tp"),
            P("ctx", "tp"),
            P("ctx", "tp"),
            P("ctx", None, "tp"),
            P("ctx", None, "tp"),
            P("ctx", None, None),
            P("ctx", None),
            P("ctx"),
            P("tp", "ctx"),
        ),
        out_specs=P("tp", "ctx"),
        check_vma=False,
    )
```
